512 devices in a mesh: ctx: 64 (over y, z_lo, core), fsdp: 8 (over z_hi, x).
Axes of the slice: x: 4, y: 8, z: 8 (z_hi: 2, z_lo: 4; z = z_hi * 4 + z_lo), core: 2. Of those that a mesh axis runs over, the one named last changes fastest.
Arguments:
- tokens: bfloat16 [16384, 8192], P('ctx'), may hold values from -6 to 6
- query_weight: bfloat16 [8192, 4096], P('ctx', 'fsdp'), may hold values from -0.0625 to 0.0625
- key_weight: bfloat16 [8192, 1024], P('ctx', 'fsdp'), may hold values from -0.0625 to 0.0625
- value_weight: bfloat16 [8192, 1024], P('ctx', 'fsdp'), may hold values from -0.0625 to 0.0625
- adapter_down_weight: bfloat16 [8192, 32], P('ctx'), may hold values from -0.0625 to 0.0625
- query_up_weight: bfloat16 [16, 4096], P(None, 'fsdp'), may hold values from -1.5 to 1.5
- value_up_weight: bfloat16 [16, 1024], P(None, 'fsdp'), may hold values from -1.5 to 1.5
- head_shifts: int32 [32], P('fsdp'), may hold values from 0 to 1024, as said below
- output_gradient: bfloat16 [16384, 4096], P('ctx', 'fsdp'), may hold values from -6 to 6
Outputs:
- attention: bfloat16 [16384, 4096], P('ctx', 'fsdp')
- value_gradient: bfloat16 [16384, 1024], P('ctx', 'fsdp')
- grad_down: float32 [8192, 32], P('ctx')
- query_up_gradient: float32 [16, 4096], P(None, 'fsdp')
- value_up_gradient: float32 [16, 1024], P(None, 'fsdp')
The draws below stay inside these ranges and needn't reach their ends.
Inputs may be any that keep to these rules, and one draw needn't show every extreme that they name: `head_shifts`: exactly half of the 32 heads have offset 2048 // 2, the others 0.
All inputs are finite; a program needn't handle non-finite values.
Results may differ from the reference program's by a relative error of at most 0.025.
The reference program's roundings to bfloat16 on the way count: a program that leaves them out, or rounds other values in their place, can miss the bound.
Values may be sent and summed in bfloat16 or wider, within the bound.
No kernel may reach another device: no remote copies, remote signals or barrier semaphores. Data moves between devices by JAX's collectives and lax.ppermute only.
A program may use at most 64 MiB of HBM per device.

```python
import jax
import jax.numpy as jnp
from jax import lax

MODEL_WIDTH = 8192
KEY_VALUE_HEADS = 8
HEAD_SIZE = 128
QUERY_HEADS = 32
ADAPTER_RANK = 16
GROUP = 2048
SEQ = 16384


def draw_tokens(key, part):
    key = jax.random.fold_in(key, 11)
    base_key = jax.random.fold_in(key, 0)
    value_rows = jnp.clip(jax.random.normal(base_key, (SEQ, MODEL_WIDTH), jnp.float32), -6.0, 6.0)
    return value_rows.astype(jnp.bfloat16)


def draw_head_shifts(key, part):
    key = jax.random.fold_in(key, 23)
    order = jax.random.permutation(key, QUERY_HEADS)
    return jnp.where(order < QUERY_HEADS // 2, GROUP // 2, 0).astype(jnp.int32)


def shard_levels(stream_key, shape, shards, smallest, largest):
    factor_of, own = 1.0, jax.random.fold_in(stream_key, 6)
    for dim, blocks in shards:
        draws = jnp.exp(jax.random.uniform(jax.random.fold_in(own, dim), (blocks,), jnp.float32, smallest / len(shards), largest / len(shards)))
        factor_of = factor_of * jnp.repeat(draws, shape[dim] // blocks).reshape([-1 if axis == dim else 1 for axis in range(len(shape))])
    return factor_of


def centred(key, shape, deviation, bound, cuts=(), kind=jnp.bfloat16):
    factor_of = shard_levels(key, shape, cuts, -0.22, 0.18) if cuts else 1.0
    values = jax.random.normal(key, shape, jnp.float32) * deviation * factor_of
    return jnp.minimum(jnp.maximum(values, -bound), bound).astype(kind)


def setup_inputs(seed: int = 0) -> dict:
    key_list = jax.random.split(jax.random.key(seed), 10)
    tokens = draw_tokens(jax.random.fold_in(key_list[9], 71), 0)
    query_weight = centred(key_list[1], (MODEL_WIDTH, QUERY_HEADS * HEAD_SIZE), MODEL_WIDTH ** -0.5, 0.0625, ((0, 64), (1, 8)))
    key_weight = centred(key_list[2], (MODEL_WIDTH, KEY_VALUE_HEADS * HEAD_SIZE), MODEL_WIDTH ** -0.5, 0.0625, ((0, 64), (1, 8)))
    value_weight = centred(key_list[3], (MODEL_WIDTH, KEY_VALUE_HEADS * HEAD_SIZE), MODEL_WIDTH ** -0.5, 0.0625, ((0, 64), (1, 8)))
    adapter_down_weight = centred(key_list[4], (MODEL_WIDTH, 2 * ADAPTER_RANK), MODEL_WIDTH ** -0.5, 0.0625, ((0, 64),))
    query_up_weight = centred(key_list[5], (ADAPTER_RANK, QUERY_HEADS * HEAD_SIZE), ADAPTER_RANK ** -0.5, 1.5, ((1, 8),))
    value_up_weight = centred(key_list[6], (ADAPTER_RANK, KEY_VALUE_HEADS * HEAD_SIZE), ADAPTER_RANK ** -0.5, 1.5, ((1, 8),))
    head_shifts = draw_head_shifts(jax.random.fold_in(key_list[9], 71), 0)
    output_gradient = centred(key_list[8], (SEQ, QUERY_HEADS * HEAD_SIZE), 1.0, 6.0, ((0, 64), (1, 8)))
    return {"tokens": tokens, "query_weight": query_weight, "key_weight": key_weight, "value_weight": value_weight, "adapter_down_weight": adapter_down_weight, "query_up_weight": query_up_weight, "value_up_weight": value_up_weight, "head_shifts": head_shifts, "output_gradient": output_gradient}


adapter_scale = 1.0


def masked_softmax(logits, allowed):
    shifted = jnp.where(allowed, logits, -1e30)
    highest = jnp.max(shifted, axis=-1, keepdims=True)
    weights = jnp.where(allowed, jnp.exp(shifted - highest), 0.0)
    return weights / jnp.sum(weights, axis=-1, keepdims=True)


def reference(tokens, query_weight, key_weight, value_weight, adapter_down_weight, query_up_weight, value_up_weight, head_shifts, output_gradient):
    score_scale = HEAD_SIZE ** -0.5
    repeat = QUERY_HEADS // KEY_VALUE_HEADS
    groups = SEQ // GROUP
    reduced_activations = jnp.dot(tokens, adapter_down_weight, preferred_element_type=jnp.float32).astype(jnp.bfloat16)
    query_reduced = reduced_activations[:, :ADAPTER_RANK]
    value_reduced = reduced_activations[:, ADAPTER_RANK:]
    query_matrix = (jnp.dot(tokens, query_weight, preferred_element_type=jnp.float32) + adapter_scale * jnp.dot(query_reduced, query_up_weight, preferred_element_type=jnp.float32)).astype(jnp.bfloat16)
    keys = jnp.dot(tokens, key_weight, preferred_element_type=jnp.float32).astype(jnp.bfloat16)
    value_rows = (jnp.dot(tokens, value_weight, preferred_element_type=jnp.float32) + adapter_scale * jnp.dot(value_reduced, value_up_weight, preferred_element_type=jnp.float32)).astype(jnp.bfloat16)
    query_heads = query_matrix.reshape(SEQ, QUERY_HEADS, HEAD_SIZE).transpose(1, 0, 2)
    grad_heads = output_gradient.reshape(SEQ, QUERY_HEADS, HEAD_SIZE).transpose(1, 0, 2)
    key_heads = keys.reshape(SEQ, KEY_VALUE_HEADS, HEAD_SIZE).transpose(1, 0, 2)
    value_heads = value_rows.reshape(SEQ, KEY_VALUE_HEADS, HEAD_SIZE).transpose(1, 0, 2)
    causal = jnp.tril(jnp.ones((GROUP, GROUP), dtype=bool))

    def one_head(head_items):
        query_one, grad_one, offset, pair_index = head_items
        key_one = key_heads[pair_index]
        value_one = value_heads[pair_index]

        def rolled(tensor):
            return jnp.roll(tensor, -offset, axis=0).reshape(groups, GROUP, HEAD_SIZE).astype(jnp.float32)

        def unrolled(tensor):
            return jnp.roll(tensor.reshape(SEQ, HEAD_SIZE), offset, axis=0)

        query_rolled = rolled(query_one)
        key_rolled = rolled(key_one)
        value_rolled = rolled(value_one)
        grad_rolled = rolled(grad_one)
        scores = jnp.einsum("ntd,nsd->nts", query_rolled, key_rolled)
        attn_weights = masked_softmax(scores * score_scale, causal)
        weights_low = attn_weights.astype(jnp.bfloat16)
        output = jnp.einsum("nts,nsd->ntd", weights_low.astype(jnp.float32), value_rolled).astype(jnp.bfloat16)
        grad_weights = jnp.einsum("ntd,nsd->nts", grad_rolled, value_rolled)
        correction = jnp.sum(grad_rolled * output.astype(jnp.float32), axis=-1)
        grad_scores = (attn_weights * (grad_weights - correction[..., None])).astype(jnp.bfloat16)
        grad_query_one = (jnp.einsum("nts,nsd->ntd", grad_scores.astype(jnp.float32), key_rolled) * score_scale).astype(jnp.bfloat16)
        value_part = jnp.einsum("nts,ntd->nsd", weights_low.astype(jnp.float32), grad_rolled)
        return unrolled(output), unrolled(grad_query_one), unrolled(value_part)

    pair_indices = jnp.arange(QUERY_HEADS, dtype=jnp.int32) // repeat
    outputs, grad_query_heads, value_parts = lax.map(one_head, (query_heads, grad_heads, head_shifts, pair_indices))
    attention = outputs.transpose(1, 0, 2).reshape(SEQ, QUERY_HEADS * HEAD_SIZE)
    query_gradient = grad_query_heads.transpose(1, 0, 2).reshape(SEQ, QUERY_HEADS * HEAD_SIZE)
    value_gradient = value_parts.reshape(KEY_VALUE_HEADS, repeat, SEQ, HEAD_SIZE).sum(axis=1).astype(jnp.bfloat16)
    value_gradient = value_gradient.transpose(1, 0, 2).reshape(SEQ, KEY_VALUE_HEADS * HEAD_SIZE)
    rank_terms = jnp.concatenate([
        adapter_scale * jnp.dot(query_gradient, query_up_weight.T, preferred_element_type=jnp.float32),
        adapter_scale * jnp.dot(value_gradient, value_up_weight.T, preferred_element_type=jnp.float32)], axis=1)
    rank_grad = rank_terms.astype(jnp.bfloat16)
    grad_down = jnp.dot(tokens.T, rank_grad, preferred_element_type=jnp.float32)
    query_up_gradient = adapter_scale * jnp.dot(query_reduced.T, query_gradient, preferred_element_type=jnp.float32)
    value_up_gradient = adapter_scale * jnp.dot(value_reduced.T, value_gradient, preferred_element_type=jnp.float32)
    return (attention, value_gradient, grad_down, query_up_gradient, value_up_gradient)
```

```python
import jax
import jax.numpy as jnp
from jax import lax
from jax.sharding import PartitionSpec as P

GROUP = 2048
bf16 = jnp.bfloat16
f32 = jnp.float32


def groups_of(devices, members):
    half = members // 2
    plain = [[start + i for i in range(members)] for start in range(0, devices, members)]
    shifted = [
        [(start + half + i) % devices for i in range(members)]
        for start in range(0, devices, members)
    ]
    return plain, shifted


def spread(value, axis, groups=None):
    count = len(groups[0]) if groups else lax.axis_size(axis)
    copies = jnp.broadcast_to(value[None], (count, *value.shape))
    return lax.all_to_all(copies, axis, 0, 0, tiled=True, axis_index_groups=groups)


def on_device(
    tokens,
    query_weight,
    key_weight,
    value_weight,
    adapter_down_weight,
    query_up_weight,
    value_up_weight,
    head_shifts,
    output_gradient,
):
    rows = tokens.shape[0]
    heads = head_shifts.shape[0]
    width = query_weight.shape[1]
    size = width // heads
    rank = adapter_down_weight.shape[1] // 2
    devices = lax.axis_size("ctx")
    members = GROUP // rows
    scale = size ** (-0.5)
    position = lax.axis_index("ctx")
    plain, shifted = groups_of(devices, members)
    across = [[g[i] for g in plain] for i in range(members)]

    packed = jnp.concatenate(
        [query_weight, key_weight, value_weight, adapter_down_weight], axis=1
    )
    gathered = lax.all_gather(packed, "ctx", axis=0, tiled=True)
    projected = jnp.dot(tokens, gathered, preferred_element_type=f32)
    low = projected[:, width + 2 * size :].astype(bf16)
    low_q, low_v = low[:, :rank], low[:, rank:]
    query = (
        projected[:, :width] + jnp.dot(low_q, query_up_weight, preferred_element_type=f32)
    ).astype(bf16)
    keys = projected[:, width : width + size].astype(bf16)
    values = (
        projected[:, width + size : width + 2 * size]
        + jnp.dot(low_v, value_up_weight, preferred_element_type=f32)
    ).astype(bf16)
    pair = jnp.stack([keys, values])
    kv = jnp.stack([spread(pair, "ctx", plain), spread(pair, "ctx", shifted)])
    kv = kv.transpose(0, 2, 1, 3, 4).reshape(2, 2, GROUP, size)

    moved = head_shifts != 0
    key_heads = jnp.where(moved[:, None, None], kv[1, 0], kv[0, 0])
    value_heads = jnp.where(moved[:, None, None], kv[1, 1], kv[0, 1])
    place = jnp.where(moved, (position + members // 2) % members, position % members)
    row = place[:, None] * rows + jnp.arange(rows, dtype=jnp.int32)
    allowed = jnp.arange(GROUP, dtype=jnp.int32)[None, None, :] <= row[:, :, None]
    query_heads = query.reshape(rows, heads, size)
    grad_heads = output_gradient.reshape(rows, heads, size)
    scores = jnp.einsum("thd,hld->htl", query_heads, key_heads, preferred_element_type=f32)
    scores = jnp.where(allowed, scores * scale, -1e30)
    weights = jnp.exp(scores - jnp.max(scores, axis=-1, keepdims=True))
    weights = jnp.where(allowed, weights, 0.0)
    weights = weights / jnp.sum(weights, axis=-1, keepdims=True)
    weights_low = weights.astype(bf16)
    output = jnp.einsum(
        "htl,hld->thd", weights_low, value_heads, preferred_element_type=f32
    ).astype(bf16)
    grad_weights = jnp.einsum(
        "thd,hld->htl", grad_heads, value_heads, preferred_element_type=f32
    )
    correction = jnp.sum(grad_heads.astype(f32) * output.astype(f32), axis=-1).T
    grad_scores = (weights * (grad_weights - correction[..., None])).astype(bf16)
    grad_query = (
        jnp.einsum("htl,hld->thd", grad_scores, key_heads, preferred_element_type=f32) * scale
    ).astype(bf16)
    grad_query = grad_query.reshape(rows, width)
    value_parts = jnp.einsum(
        "htl,thd->hld", weights_low, grad_heads, preferred_element_type=f32
    )

    query_up_part = lax.dot_general(
        low_q, grad_query, (((0,), (0,)), ((), ())), preferred_element_type=f32
    ).astype(bf16)
    query_up_part = jnp.sum(spread(query_up_part, "ctx", across).astype(f32), axis=0).astype(bf16)
    query_up_gradient = jnp.sum(spread(query_up_part, "ctx", plain).astype(f32), axis=0)

    value_gradient = 0.0
    for groups, mine in ((plain, ~moved), (shifted, moved)):
        part = jnp.sum(jnp.where(mine[:, None, None], value_parts, 0.0), axis=0)
        part = part.astype(bf16).reshape(members, rows, size)
        arrived = lax.all_to_all(part, "ctx", 0, 0, tiled=True, axis_index_groups=groups)
        value_gradient = value_gradient + jnp.sum(arrived.astype(f32), axis=0)
    value_gradient = value_gradient.astype(bf16)

    rank_terms = jnp.concatenate(
        [
            jnp.dot(grad_query, query_up_weight.T, preferred_element_type=f32),
            jnp.dot(value_gradient, value_up_weight.T, preferred_element_type=f32),
        ],
        axis=1,
    ).astype(bf16)
    rank_grad = jnp.sum(spread(rank_terms, "fsdp").astype(f32), axis=0).astype(bf16)
    grad_down = lax.dot_general(
        rank_grad, tokens, (((0,), (0,)), ((), ())), preferred_element_type=f32
    ).astype(bf16)
    grad_down = grad_down.reshape(2 * rank, devices, -1).transpose(1, 0, 2)
    value_up_part = lax.dot_general(
        low_v, value_gradient, (((0,), (0,)), ((), ())), preferred_element_type=f32
    ).astype(bf16)
    payload = jnp.concatenate(
        [grad_down, jnp.broadcast_to(value_up_part[None], (devices, rank, size))], axis=1
    )
    payload = lax.all_to_all(payload, "ctx", 0, 0, tiled=True)
    payload = jnp.sum(payload.astype(f32), axis=0)
    return (
        output.reshape(rows, width),
        value_gradient,
        payload[: 2 * rank].T,
        query_up_gradient,
        payload[2 * rank :],
    )


def solution(mesh):
    in_specs = (
        P("ctx", None),
        P("ctx", "fsdp"),
        P("ctx", "fsdp"),
        P("ctx", "fsdp"),
        P("ctx", None),
        P(None, "fsdp"),
        P(None, "fsdp"),
        P("fsdp"),
        P("ctx", "fsdp"),
    )
    out_specs = (
        P("ctx", "fsdp"),
        P("ctx", "fsdp"),
        P("ctx", None),
        P(None, "fsdp"),
        P(None, "fsdp"),
    )
    return jax.shard_map(
        on_device, mesh=mesh, in_specs=in_specs, out_specs=out_specs, check_vma=False
    )
```

```python
import functools

import jax
import jax.numpy as jnp
from jax import lax
from jax.experimental import pallas as pl
from jax.experimental.pallas import tpu as pltpu
from jax.sharding import PartitionSpec as P

GROUP = 2048
bf16 = jnp.bfloat16
f32 = jnp.float32
NT = (((1,), (1,)), ((), ()))
TN = (((0,), (0,)), ((), ()))


def spread(value, axis, groups=None):
    count = len(groups[0]) if groups else lax.axis_size(axis)
    copies = jnp.broadcast_to(value[None], (count, *value.shape))
    return lax.all_to_all(copies, axis, 0, 0, tiled=True, axis_index_groups=groups)


def to_chip(value, chips, other_core):
    count = lax.axis_size("ctx")
    pairs = []
    for source in range(count):
        core = source % 2
        target = (source - core + 2 * chips) % count + (1 - core if other_core else core)
        pairs.append((source, target))
    return lax.ppermute(value, "ctx", pairs)


def attention_kernel(
    scale, tile, info, query, grad_out, kv, out, grad_query, grad_value, probs, acc, stat
):
    rows, size = query.shape[0], kv.shape[-1]
    heads = query.shape[1] // size
    block = kv.shape[2]
    key_slot = info[heads]
    value_slot = 1 - key_slot
    lanes = 128
    grad_value[...] = jnp.zeros_like(grad_value)

    def fold(values, op):
        total = values[:, :lanes]
        for start in range(lanes, values.shape[1], lanes):
            total = op(total, values[:, start : start + lanes])
        return total

    for head in range(heads):
        columns = slice(head * size, (head + 1) * size)
        seen = info[head] + 1

        def one_tile(index, carry, columns=columns, seen=seen):
            here = pl.ds(pl.multiple_of(index * tile, tile), tile)
            q = query[here, columns]
            do = grad_out[here, columns]

            def score(d):
                return lax.dot_general(
                    q, kv[key_slot, d], NT, preferred_element_type=f32
                ) * scale

            row = index * tile + lax.broadcasted_iota(jnp.int32, (tile, block), 0)
            column = lax.broadcasted_iota(jnp.int32, (tile, block), 1)
            own = jnp.where(column <= row, score(0), -1e30)
            probs[0] = own
            stat[...] = fold(own, jnp.maximum)

            def first(d, carry):
                s = score(d)
                probs[d] = s
                stat[...] = jnp.maximum(stat[...], fold(s, jnp.maximum))
                return carry

            lax.fori_loop(1, seen, first, 0)
            highest = jnp.max(stat[...], axis=1, keepdims=True)
            stat[...] = jnp.zeros_like(stat)

            def second(d, carry):
                e = jnp.exp(probs[d] - highest)
                probs[d] = e
                stat[...] += fold(e, jnp.add)
                return carry

            lax.fori_loop(0, seen, second, 0)
            inverse = 1.0 / jnp.sum(stat[...], axis=1, keepdims=True)
            acc[...] = jnp.zeros_like(acc)

            def third(d, carry):
                p = probs[d] * inverse
                probs[d] = p
                low = p.astype(bf16)
                acc[...] += jnp.dot(low, kv[value_slot, d], preferred_element_type=f32)
                grad_value[d] += lax.dot_general(low, do, TN, preferred_element_type=f32)
                return carry

            lax.fori_loop(0, seen, third, 0)
            result = acc[...].astype(bf16)
            out[here, columns] = result
            correction = jnp.sum(do.astype(f32) * result.astype(f32), axis=1, keepdims=True)
            acc[...] = jnp.zeros_like(acc)

            def fourth(d, carry):
                dp = lax.dot_general(do, kv[value_slot, d], NT, preferred_element_type=f32)
                ds = (probs[d] * (dp - correction)).astype(bf16)
                acc[...] += jnp.dot(ds, kv[key_slot, d], preferred_element_type=f32)
                return carry

            lax.fori_loop(0, seen, fourth, 0)
            grad_query[here, columns] = (acc[...] * scale).astype(bf16)
            return carry

        lax.fori_loop(0, rows // tile, one_tile, 0)


def attend(info, query, grad_out, kv, tile=256):
    rows, width = query.shape
    size = kv.shape[-1]
    blocks, block = kv.shape[1:3]
    vmem = pl.BlockSpec(memory_space=pltpu.VMEM)
    return pl.pallas_call(
        functools.partial(attention_kernel, size ** (-0.5), tile),
        out_shape=(
            jax.ShapeDtypeStruct((rows, width), bf16),
            jax.ShapeDtypeStruct((rows, width), bf16),
            jax.ShapeDtypeStruct((blocks, block, size), f32),
        ),
        in_specs=[pl.BlockSpec(memory_space=pltpu.SMEM), vmem, vmem, vmem],
        out_specs=(vmem, vmem, vmem),
        scratch_shapes=[
            pltpu.VMEM((blocks, tile, block), f32),
            pltpu.VMEM((tile, size), f32),
            pltpu.VMEM((tile, 128), f32),
        ],
        compiler_params=pltpu.CompilerParams(vmem_limit_bytes=40 * 1024 * 1024),
        cost_estimate=pl.CostEstimate(
            flops=10 * rows * width * blocks * block,
            bytes_accessed=4 * 1024 * 1024,
            transcendentals=rows * width // size * blocks * block,
        ),
        name="attention",
    )(info, query, grad_out, kv)


def on_device(
    tokens,
    query_weight,
    key_weight,
    value_weight,
    adapter_down_weight,
    query_up_weight,
    value_up_weight,
    head_shifts,
    output_gradient,
):
    rows, model = tokens.shape
    heads = head_shifts.shape[0]
    width = query_weight.shape[1]
    size = width // heads
    half = width // 2
    depth = query_weight.shape[0]
    rank = adapter_down_weight.shape[1] // 2
    devices = lax.axis_size("ctx")
    chips = GROUP // (2 * rows)
    members = 2 * chips
    position = lax.axis_index("ctx")
    core = position % 2
    chip = position // 2 % chips
    plain = [[start + i for i in range(members)] for start in range(0, devices, members)]
    across = [[g[i] for g in plain] for i in range(members)]
    planes = devices // members

    def both(mine, theirs):
        return jnp.concatenate(
            [jnp.where(core == 0, mine, theirs), jnp.where(core == 0, theirs, mine)], axis=0
        )

    def half_of(array, which):
        return lax.dynamic_slice_in_dim(array, which * (array.shape[0] // 2), array.shape[0] // 2)

    down = adapter_down_weight.T
    kv_rows = jnp.stack(
        [jnp.concatenate([key_weight, down]), jnp.concatenate([value_weight, down])]
    )
    kv_rows = jnp.broadcast_to(kv_rows[None], (chips, *kv_rows.shape))
    kv_rows = lax.all_to_all(
        kv_rows.reshape(members, depth + 2 * rank, size),
        "ctx", 0, 0, tiled=True, axis_index_groups=plain,
    )
    kv_rows = lax.all_gather(kv_rows, "ctx", axis=0, tiled=True, axis_index_groups=across)
    q_rows = jnp.stack([query_weight[:, :half], query_weight[:, half:]])
    q_rows = jnp.broadcast_to(q_rows[None], (chips, *q_rows.shape))
    q_rows = lax.all_to_all(
        q_rows.reshape(members, depth, half),
        "ctx", 0, 0, tiled=True, axis_index_groups=plain,
    )
    q_rows = lax.all_gather(
        q_rows.reshape(members * depth, half),
        "ctx", axis=0, tiled=True, axis_index_groups=across,
    )

    chip_tokens = both(tokens, to_chip(tokens, 0, True))
    grad_halves = output_gradient.reshape(rows, 2, half).transpose(1, 0, 2)
    grad_mine = lax.dynamic_index_in_dim(grad_halves, core, 0, keepdims=False)
    grad_away = lax.dynamic_index_in_dim(grad_halves, 1 - core, 0, keepdims=False)
    grad_out = both(grad_mine, to_chip(grad_away, 0, True))

    low_weight = kv_rows[:, depth:].transpose(1, 0, 2).reshape(2 * rank, model)
    low = lax.dot_general(chip_tokens, low_weight, NT, preferred_element_type=f32).astype(bf16)
    low_q, low_v = low[:, :rank], low[:, rank:]
    mine = jnp.dot(
        chip_tokens, kv_rows[:, :depth].reshape(model, size), preferred_element_type=f32
    )
    extra = jnp.dot(low_v, value_up_weight, preferred_element_type=f32)
    mine = (mine + jnp.where(core == 1, extra, 0.0)).astype(bf16)
    kv = jnp.stack(
        [
            jnp.stack([mine] + [to_chip(mine, d, False) for d in range(1, chips)]),
            jnp.stack([to_chip(mine, d, True) for d in range(chips)]),
        ]
    )

    up_mine = lax.dynamic_slice_in_dim(query_up_weight, core * half, half, axis=1)
    query = (
        jnp.dot(chip_tokens, q_rows, preferred_element_type=f32)
        + jnp.dot(low_q, up_mine, preferred_element_type=f32)
    ).astype(bf16)

    shifts = lax.dynamic_slice_in_dim(head_shifts, core * (heads // 2), heads // 2)
    seen = jnp.where(shifts != 0, (chip + chips // 2) % chips, chip)
    info = jnp.concatenate([seen, core[None]]).astype(jnp.int32)
    output, grad_query, value_parts = attend(info, query, grad_out, kv)

    attention_mine = half_of(output, core)
    attention_other = to_chip(half_of(output, 1 - core), 0, True)
    attention = jnp.concatenate(
        [
            jnp.where(core == 0, attention_mine, attention_other),
            jnp.where(core == 0, attention_other, attention_mine),
        ],
        axis=1,
    )

    value_parts = value_parts.reshape(chips, 2, rows, size).astype(bf16)
    same = lax.dynamic_index_in_dim(value_parts, core, 1, keepdims=False)
    cross = lax.dynamic_index_in_dim(value_parts, 1 - core, 1, keepdims=False)
    arrived = [same[0]]
    arrived += [to_chip(cross[d], -d, True) for d in range(chips)]
    arrived += [to_chip(same[d], -d, False) for d in range(1, chips)]
    value_gradient = functools.reduce(jnp.add, [a.astype(f32) for a in arrived]).astype(bf16)

    query_up_part = lax.dot_general(low_q, grad_query, TN, preferred_element_type=f32)
    query_up_part = query_up_part.astype(bf16).reshape(planes, rank // planes, half)
    query_up_part = lax.all_to_all(
        query_up_part, "ctx", 0, 0, tiled=True, axis_index_groups=across
    )
    query_up_part = jnp.sum(
        query_up_part.reshape(planes, rank // planes, half).astype(f32), axis=0
    ).astype(bf16)

    rank_q = lax.dot_general(grad_query, up_mine, NT, preferred_element_type=f32)
    rank_q = half_of(rank_q, core) + to_chip(half_of(rank_q, 1 - core), 0, True)
    rank_v = lax.dot_general(value_gradient, value_up_weight, NT, preferred_element_type=f32)
    rank_terms = jnp.concatenate([rank_q, rank_v], axis=1).astype(bf16)
    rank_grad = jnp.sum(spread(rank_terms, "fsdp").astype(f32), axis=0).astype(bf16)
    grad_down = lax.dot_general(rank_grad, tokens, TN, preferred_element_type=f32)
    grad_down = grad_down.astype(bf16).reshape(2 * rank, devices, depth).transpose(1, 0, 2)
    value_up_part = lax.dot_general(
        half_of(low_v, core), value_gradient, TN, preferred_element_type=f32
    ).astype(bf16)
    shared = jnp.concatenate(
        [value_up_part, query_up_part.reshape(-1, size)], axis=0
    )
    payload = jnp.concatenate(
        [grad_down, jnp.broadcast_to(shared[None], (devices, *shared.shape))], axis=1
    )
    payload = lax.all_to_all(payload, "ctx", 0, 0, tiled=True)
    summed = jnp.sum(payload[:, : 3 * rank].astype(f32), axis=0)
    query_up = payload[:, 3 * rank :].astype(f32)
    query_up = query_up.reshape(planes, chips, 2, rank // planes, half).sum(axis=1)
    query_up_gradient = query_up.transpose(0, 2, 1, 3).reshape(rank, width)
    return (
        attention,
        value_gradient,
        summed[: 2 * rank].T,
        query_up_gradient,
        summed[2 * rank :],
    )


def solution(mesh):
    in_specs = (
        P("ctx", None),
        P("ctx", "fsdp"),
        P("ctx", "fsdp"),
        P("ctx", "fsdp"),
        P("ctx", None),
        P(None, "fsdp"),
        P(None, "fsdp"),
        P("fsdp"),
        P("ctx", "fsdp"),
    )
    out_specs = (
        P("ctx", "fsdp"),
        P("ctx", "fsdp"),
        P("ctx", None),
        P(None, "fsdp"),
        P(None, "fsdp"),
    )
    return jax.shard_map(
        on_device, mesh=mesh, in_specs=in_specs, out_specs=out_specs, check_vma=False
    )
```

```python
import functools

import jax
import jax.numpy as jnp
from jax import lax
from jax.experimental import pallas as pl
from jax.experimental.pallas import tpu as pltpu
from jax.sharding import PartitionSpec as P

GROUP = 2048
bf16 = jnp.bfloat16
f32 = jnp.float32
NT = (((1,), (1,)), ((), ()))
TN = (((0,), (0,)), ((), ()))


def spread(value, axis, groups=None):
    count = len(groups[0]) if groups else lax.axis_size(axis)
    copies = jnp.broadcast_to(value[None], (count, *value.shape))
    return lax.all_to_all(copies, axis, 0, 0, tiled=True, axis_index_groups=groups)


def to_chip(value, chips, other_core):
    count = lax.axis_size("ctx")
    pairs = []
    for source in range(count):
        core = source % 2
        target = (source - core + 2 * chips) % count + (1 - core if other_core else core)
        pairs.append((source, target))
    return lax.ppermute(value, "ctx", pairs)


def attention_kernel(
    scale, tile, info, query, grad_out, kv, out, grad_query, grad_value, probs, acc, stat
):
    rows, size = query.shape[0], kv.shape[-1]
    heads = query.shape[1] // size
    block = kv.shape[2]
    key_slot = info[heads]
    value_slot = 1 - key_slot
    lanes = 128
    grad_value[...] = jnp.zeros_like(grad_value)

    def fold(values, op):
        total = values[:, :lanes]
        for start in range(lanes, values.shape[1], lanes):
            total = op(total, values[:, start : start + lanes])
        return total

    for head in range(heads):
        columns = slice(head * size, (head + 1) * size)
        seen = info[head] + 1

        def one_tile(index, carry, columns=columns, seen=seen):
            here = pl.ds(pl.multiple_of(index * tile, tile), tile)
            q = query[here, columns]
            do = grad_out[here, columns]

            def score(d):
                return lax.dot_general(
                    q, kv[key_slot, d], NT, preferred_element_type=f32
                ) * scale

            row = index * tile + lax.broadcasted_iota(jnp.int32, (tile, block), 0)
            column = lax.broadcasted_iota(jnp.int32, (tile, block), 1)
            own = jnp.where(column <= row, score(0), -1e30)
            probs[0] = own
            stat[...] = fold(own, jnp.maximum)

            def first(d, carry):
                s = score(d)
                probs[d] = s
                stat[...] = jnp.maximum(stat[...], fold(s, jnp.maximum))
                return carry

            lax.fori_loop(1, seen, first, 0)
            highest = jnp.max(stat[...], axis=1, keepdims=True)
            stat[...] = jnp.zeros_like(stat)

            def second(d, carry):
                e = jnp.exp(probs[d] - highest)
                probs[d] = e
                stat[...] += fold(e, jnp.add)
                return carry

            lax.fori_loop(0, seen, second, 0)
            inverse = 1.0 / jnp.sum(stat[...], axis=1, keepdims=True)
            acc[...] = jnp.zeros_like(acc)

            def third(d, carry):
                p = probs[d] * inverse
                probs[d] = p
                low = p.astype(bf16)
                acc[...] += jnp.dot(low, kv[value_slot, d], preferred_element_type=f32)
                grad_value[d] += lax.dot_general(low, do, TN, preferred_element_type=f32)
                return carry

            lax.fori_loop(0, seen, third, 0)
            result = acc[...].astype(bf16)
            out[here, columns] = result
            correction = jnp.sum(do.astype(f32) * result.astype(f32), axis=1, keepdims=True)
            acc[...] = jnp.zeros_like(acc)

            def fourth(d, carry):
                dp = lax.dot_general(do, kv[value_slot, d], NT, preferred_element_type=f32)
                ds = (probs[d] * (dp - correction)).astype(bf16)
                acc[...] += jnp.dot(ds, kv[key_slot, d], preferred_element_type=f32)
                return carry

            lax.fori_loop(0, seen, fourth, 0)
            grad_query[here, columns] = (acc[...] * scale).astype(bf16)
            return carry

        lax.fori_loop(0, rows // tile, one_tile, 0)


def attend(info, query, grad_out, kv, tile=256):
    rows, width = query.shape
    size = kv.shape[-1]
    blocks, block = kv.shape[1:3]
    vmem = pl.BlockSpec(memory_space=pltpu.VMEM)
    return pl.pallas_call(
        functools.partial(attention_kernel, size ** (-0.5), tile),
        out_shape=(
            jax.ShapeDtypeStruct((rows, width), bf16),
            jax.ShapeDtypeStruct((rows, width), bf16),
            jax.ShapeDtypeStruct((blocks, block, size), f32),
        ),
        in_specs=[pl.BlockSpec(memory_space=pltpu.SMEM), vmem, vmem, vmem],
        out_specs=(vmem, vmem, vmem),
        scratch_shapes=[
            pltpu.VMEM((blocks, tile, block), f32),
            pltpu.VMEM((tile, size), f32),
            pltpu.VMEM((tile, 128), f32),
        ],
        compiler_params=pltpu.CompilerParams(vmem_limit_bytes=40 * 1024 * 1024),
        cost_estimate=pl.CostEstimate(
            flops=10 * rows * width * blocks * block,
            bytes_accessed=4 * 1024 * 1024,
            transcendentals=rows * width // size * blocks * block,
        ),
        name="attention",
    )(info, query, grad_out, kv)


def on_device(
    tokens,
    query_weight,
    key_weight,
    value_weight,
    adapter_down_weight,
    query_up_weight,
    value_up_weight,
    head_shifts,
    output_gradient,
):
    rows, model = tokens.shape
    heads = head_shifts.shape[0]
    width = query_weight.shape[1]
    size = width // heads
    half = width // 2
    depth = query_weight.shape[0]
    rank = adapter_down_weight.shape[1] // 2
    devices = lax.axis_size("ctx")
    chips = GROUP // (2 * rows)
    members = 2 * chips
    position = lax.axis_index("ctx")
    core = position % 2
    chip = position // 2 % chips
    plain = [[start + i for i in range(members)] for start in range(0, devices, members)]
    across = [[g[i] for g in plain] for i in range(members)]
    planes = devices // members

    def both(mine, theirs):
        return jnp.concatenate(
            [jnp.where(core == 0, mine, theirs), jnp.where(core == 0, theirs, mine)], axis=0
        )

    def half_of(array, which):
        return lax.dynamic_slice_in_dim(array, which * (array.shape[0] // 2), array.shape[0] // 2)

    down = adapter_down_weight.T
    kv_rows = jnp.stack(
        [jnp.concatenate([key_weight, down]), jnp.concatenate([value_weight, down])]
    )
    kv_rows = jnp.broadcast_to(kv_rows[None], (chips, *kv_rows.shape))
    kv_rows = lax.all_to_all(
        kv_rows.reshape(members, depth + 2 * rank, size),
        "ctx", 0, 0, tiled=True, axis_index_groups=plain,
    )
    kv_rows = lax.all_gather(kv_rows, "ctx", axis=0, tiled=True, axis_index_groups=across)
    q_rows = jnp.stack([query_weight[:, :half], query_weight[:, half:]])
    q_rows = jnp.broadcast_to(q_rows[None], (chips, *q_rows.shape))
    q_rows = lax.all_to_all(
        q_rows.reshape(members, depth, half),
        "ctx", 0, 0, tiled=True, axis_index_groups=plain,
    )
    q_rows = q_rows.reshape(members * depth, half)
    ahead, back = [q_rows], [q_rows]
    for _ in range(planes // 2 - 1):
        ahead.append(to_chip(ahead[-1], chips, False))
        back.append(to_chip(back[-1], -chips, False))
    cut = members * depth // 2
    opposite = jnp.concatenate(
        [to_chip(ahead[-1][:cut], chips, False), to_chip(back[-1][cut:], -chips, False)]
    )

    chip_tokens = both(tokens, to_chip(tokens, 0, True))
    grad_halves = output_gradient.reshape(rows, 2, half).transpose(1, 0, 2)
    grad_mine = lax.dynamic_index_in_dim(grad_halves, core, 0, keepdims=False)
    grad_away = lax.dynamic_index_in_dim(grad_halves, 1 - core, 0, keepdims=False)
    grad_out = both(grad_mine, to_chip(grad_away, 0, True))

    low_weight = kv_rows[:, depth:].transpose(1, 0, 2).reshape(2 * rank, model)
    low = lax.dot_general(chip_tokens, low_weight, NT, preferred_element_type=f32).astype(bf16)
    low_q, low_v = low[:, :rank], low[:, rank:]
    mine = jnp.dot(
        chip_tokens, kv_rows[:, :depth].reshape(model, size), preferred_element_type=f32
    )
    extra = jnp.dot(low_v, value_up_weight, preferred_element_type=f32)
    mine = (mine + jnp.where(core == 1, extra, 0.0)).astype(bf16)
    mine = jnp.stack([mine] + [to_chip(mine, d, False) for d in range(1, chips)])
    kv = jnp.stack([mine, to_chip(mine, 0, True)])

    up_mine = lax.dynamic_slice_in_dim(query_up_weight, core * half, half, axis=1)
    plane = position // members
    query = jnp.dot(low_q, up_mine, preferred_element_type=f32)
    chunks = [(0, q_rows)]
    for step in range(1, planes // 2):
        chunks += [(-step, ahead[step]), (step, back[step])]
    for step, chunk in chunks + [(planes // 2, opposite)]:
        start = (plane + step) % planes * (members * depth)
        part = lax.dynamic_slice_in_dim(chip_tokens, start, members * depth, axis=1)
        query = query + jnp.dot(part, chunk, preferred_element_type=f32)
    query = query.astype(bf16)

    shifts = lax.dynamic_slice_in_dim(head_shifts, core * (heads // 2), heads // 2)
    seen = jnp.where(shifts != 0, (chip + chips // 2) % chips, chip)
    info = jnp.concatenate([seen, core[None]]).astype(jnp.int32)
    output, grad_query, value_parts = attend(info, query, grad_out, kv)

    attention_mine = half_of(output, core)
    attention_other = to_chip(half_of(output, 1 - core), 0, True)
    attention = jnp.concatenate(
        [
            jnp.where(core == 0, attention_mine, attention_other),
            jnp.where(core == 0, attention_other, attention_mine),
        ],
        axis=1,
    )

    value_parts = value_parts.reshape(chips, 2, rows, size).astype(bf16)
    same = lax.dynamic_index_in_dim(value_parts, core, 1, keepdims=False)
    cross = lax.dynamic_index_in_dim(value_parts, 1 - core, 1, keepdims=False)
    value_parts = same.astype(f32) + to_chip(cross, 0, True).astype(f32)
    arrived = [value_parts[0]]
    arrived += [to_chip(value_parts[d].astype(bf16), -d, False) for d in range(1, chips)]
    value_gradient = functools.reduce(jnp.add, [a.astype(f32) for a in arrived]).astype(bf16)

    query_up_part = lax.dot_general(low_q, grad_query, TN, preferred_element_type=f32)
    query_up_part = query_up_part.astype(bf16).reshape(planes, rank // planes, half)
    query_up_part = lax.all_to_all(
        query_up_part, "ctx", 0, 0, tiled=True, axis_index_groups=across
    )
    query_up_part = jnp.sum(
        query_up_part.reshape(planes, rank // planes, half).astype(f32), axis=0
    ).astype(bf16)

    rank_q = lax.dot_general(grad_query, up_mine, NT, preferred_element_type=f32)
    rank_q = half_of(rank_q, core) + to_chip(half_of(rank_q, 1 - core), 0, True)
    rank_v = lax.dot_general(value_gradient, value_up_weight, NT, preferred_element_type=f32)
    rank_terms = jnp.concatenate([rank_q, rank_v], axis=1).astype(bf16)
    rank_grad = jnp.sum(spread(rank_terms, "fsdp").astype(f32), axis=0).astype(bf16)
    grad_down = lax.dot_general(rank_grad, tokens, TN, preferred_element_type=f32)
    grad_down = grad_down.astype(bf16).reshape(2 * rank, devices, depth).transpose(1, 0, 2)
    value_up_part = lax.dot_general(
        half_of(low_v, core), value_gradient, TN, preferred_element_type=f32
    ).astype(bf16)
    shared = jnp.concatenate(
        [value_up_part, query_up_part.reshape(-1, size)], axis=0
    )
    payload = jnp.concatenate(
        [grad_down, jnp.broadcast_to(shared[None], (devices, *shared.shape))], axis=1
    )
    payload = lax.all_to_all(payload, "ctx", 0, 0, tiled=True)
    summed = jnp.sum(payload[:, : 3 * rank].astype(f32), axis=0)
    query_up = payload[:, 3 * rank :].astype(f32)
    query_up = query_up.reshape(planes, chips, 2, rank // planes, half).sum(axis=1)
    query_up_gradient = query_up.transpose(0, 2, 1, 3).reshape(rank, width)
    return (
        attention,
        value_gradient,
        summed[: 2 * rank].T,
        query_up_gradient,
        summed[2 * rank :],
    )


def solution(mesh):
    in_specs = (
        P("ctx", None),
        P("ctx", "fsdp"),
        P("ctx", "fsdp"),
        P("ctx", "fsdp"),
        P("ctx", None),
        P(None, "fsdp"),
        P(None, "fsdp"),
        P("fsdp"),
        P("ctx", "fsdp"),
    )
    out_specs = (
        P("ctx", "fsdp"),
        P("ctx", "fsdp"),
        P("ctx", None),
        P(None, "fsdp"),
        P(None, "fsdp"),
    )
    return jax.shard_map(
        on_device, mesh=mesh, in_specs=in_specs, out_specs=out_specs, check_vma=False
    )
```

```python
import functools

import jax
import jax.numpy as jnp
from jax import lax
from jax.experimental import pallas as pl
from jax.experimental.pallas import tpu as pltpu
from jax.sharding import PartitionSpec as P

GROUP = 2048
bf16 = jnp.bfloat16
f32 = jnp.float32
NT = (((1,), (1,)), ((), ()))
TN = (((0,), (0,)), ((), ()))


def spread(value, axis, groups=None):
    count = len(groups[0]) if groups else lax.axis_size(axis)
    copies = jnp.broadcast_to(value[None], (count, *value.shape))
    return lax.all_to_all(copies, axis, 0, 0, tiled=True, axis_index_groups=groups)


def to_chip(value, chips, other_core):
    count = lax.axis_size("ctx")
    pairs = []
    for source in range(count):
        core = source % 2
        target = (source - core + 2 * chips) % count + (1 - core if other_core else core)
        pairs.append((source, target))
    return lax.ppermute(value, "ctx", pairs)


def attention_kernel(scale, tile, info, query, grad_out, kv, out, grad_query, grad_value):
    rows, size = query.shape[0], kv.shape[-1]
    heads = query.shape[1] // size
    blocks, block = kv.shape[1:3]
    keys = [kv.at[info[heads], d] for d in range(blocks)]
    values = [kv.at[1 - info[heads], d] for d in range(blocks)]
    grad_value[...] = jnp.zeros_like(grad_value)

    def tile_of(index, columns, count):
        here = pl.ds(pl.multiple_of(index * tile, tile), tile)
        q = query[here, columns]
        do = grad_out[here, columns]
        row = index * tile + lax.broadcasted_iota(jnp.int32, (tile, block), 0)
        column = lax.broadcasted_iota(jnp.int32, (tile, block), 1)
        scores = [
            lax.dot_general(q, keys[d][...], NT, preferred_element_type=f32) * scale
            for d in range(count)
        ]
        scores[0] = jnp.where(column <= row, scores[0], -1e30)
        highest = functools.reduce(
            jnp.maximum, [jnp.max(s, axis=1, keepdims=True) for s in scores]
        )
        weights = [jnp.exp(s - highest) for s in scores]
        inverse = 1.0 / functools.reduce(
            jnp.add, [jnp.sum(w, axis=1, keepdims=True) for w in weights]
        )
        probs = [w * inverse for w in weights]
        low = [p.astype(bf16) for p in probs]
        result = functools.reduce(
            jnp.add,
            [
                jnp.dot(low[d], values[d][...], preferred_element_type=f32)
                for d in range(count)
            ],
        ).astype(bf16)
        out[here, columns] = result
        correction = jnp.sum(do.astype(f32) * result.astype(f32), axis=1, keepdims=True)
        total = jnp.zeros((tile, size), f32)
        for d in range(count):
            grad_value[d] += lax.dot_general(low[d], do, TN, preferred_element_type=f32)
            grad_probs = lax.dot_general(do, values[d][...], NT, preferred_element_type=f32)
            grad_scores = (probs[d] * (grad_probs - correction)).astype(bf16)
            total = total + jnp.dot(grad_scores, keys[d][...], preferred_element_type=f32)
        grad_query[here, columns] = (total * scale).astype(bf16)

    for head in range(heads):
        columns = slice(head * size, (head + 1) * size)
        for count in range(1, blocks + 1):

            @pl.when(info[head] + 1 == count)
            def _(columns=columns, count=count):
                def step(index, carry):
                    tile_of(index, columns, count)
                    return carry

                lax.fori_loop(0, rows // tile, step, 0)


def attend(info, query, grad_out, kv, tile=256):
    rows, width = query.shape
    size = kv.shape[-1]
    blocks, block = kv.shape[1:3]
    vmem = pl.BlockSpec(memory_space=pltpu.VMEM)
    return pl.pallas_call(
        functools.partial(attention_kernel, size ** (-0.5), tile),
        out_shape=(
            jax.ShapeDtypeStruct((rows, width), bf16),
            jax.ShapeDtypeStruct((rows, width), bf16),
            jax.ShapeDtypeStruct((blocks, block, size), f32),
        ),
        in_specs=[pl.BlockSpec(memory_space=pltpu.SMEM), vmem, vmem, vmem],
        out_specs=(vmem, vmem, vmem),
        compiler_params=pltpu.CompilerParams(vmem_limit_bytes=40 * 1024 * 1024),
        cost_estimate=pl.CostEstimate(
            flops=10 * rows * width * blocks * block,
            bytes_accessed=4 * 1024 * 1024,
            transcendentals=rows * width // size * blocks * block,
        ),
        name="attention",
    )(info, query, grad_out, kv)


def on_device(
    tokens,
    query_weight,
    key_weight,
    value_weight,
    adapter_down_weight,
    query_up_weight,
    value_up_weight,
    head_shifts,
    output_gradient,
):
    rows, model = tokens.shape
    heads = head_shifts.shape[0]
    width = query_weight.shape[1]
    size = width // heads
    half = width // 2
    depth = query_weight.shape[0]
    rank = adapter_down_weight.shape[1] // 2
    devices = lax.axis_size("ctx")
    chips = GROUP // (2 * rows)
    members = 2 * chips
    position = lax.axis_index("ctx")
    core = lax.rem(position, 2)
    chip = lax.rem(lax.div(position, 2), chips)
    plain = [[start + i for i in range(members)] for start in range(0, devices, members)]
    across = [[g[i] for g in plain] for i in range(members)]
    planes = devices // members

    def both(mine, theirs):
        return jnp.concatenate(
            [jnp.where(core == 0, mine, theirs), jnp.where(core == 0, theirs, mine)], axis=0
        )

    def half_of(array, which):
        return lax.dynamic_slice_in_dim(array, which * (array.shape[0] // 2), array.shape[0] // 2)

    def behind(value, *earlier):
        for other in earlier:
            value = value + (other.reshape(-1)[0] * 0).astype(value.dtype)
        return value

    def round_y(value, hold=None):
        ahead, back = [value], [value]
        for step in range(1, planes // 2):
            if hold and step in hold:
                ahead[-1] = behind(ahead[-1], *hold[step])
                back[-1] = behind(back[-1], *hold[step])
            ahead.append(to_chip(ahead[-1], chips, False))
            back.append(to_chip(back[-1], -chips, False))
        return ahead, back

    plane = lax.div(position, members)
    cut = members * depth // 2

    def project(total, ahead, back, last, weight_dim):
        chunks = [(0, 0, ahead[0])]
        for step in range(1, planes // 2):
            chunks += [(planes - step, 0, ahead[step]), (step, 0, back[step])]
        chunks += [(planes // 2, 0, last[0]), (planes // 2, cut, last[1])]
        for step, offset, chunk in chunks:
            start = lax.rem(plane + step, planes) * (members * depth) + offset
            count = chunk.shape[weight_dim]
            part = lax.dynamic_slice_in_dim(chip_tokens, start, count, axis=1)
            total = total + lax.dot_general(
                part, chunk, (((1,), (weight_dim,)), ((), ())), preferred_element_type=f32
            )
        return total

    chip_tokens = both(tokens, to_chip(tokens, 0, True))
    grad_halves = output_gradient.reshape(rows, 2, half).transpose(1, 0, 2)
    grad_mine = lax.dynamic_index_in_dim(grad_halves, core, 0, keepdims=False)
    grad_away = lax.dynamic_index_in_dim(grad_halves, 1 - core, 0, keepdims=False)
    grad_out = both(grad_mine, to_chip(grad_away, 0, True))

    down = adapter_down_weight.T
    kv_rows = jnp.stack(
        [jnp.concatenate([key_weight.T, down]), jnp.concatenate([value_weight.T, down])]
    )
    kv_rows = jnp.broadcast_to(kv_rows[None], (chips, *kv_rows.shape))
    kv_rows = lax.all_to_all(
        kv_rows.reshape(members, size + 2 * rank, depth),
        "ctx", 0, 0, tiled=True, axis_index_groups=plain,
    )
    kv_rows = kv_rows.transpose(1, 0, 2).reshape(size + 2 * rank, members * depth)
    kv_ahead, kv_back = round_y(kv_rows)
    kv_last = [
        to_chip(kv_ahead[-1][:, :cut], chips, False),
        to_chip(kv_back[-1][:, cut:], -chips, False),
    ]
    q_rows = behind(jnp.stack([query_weight[:, :half], query_weight[:, half:]]), kv_rows)
    q_rows = jnp.broadcast_to(q_rows[None], (chips, *q_rows.shape))
    q_rows = lax.all_to_all(
        q_rows.reshape(members, depth, half),
        "ctx", 0, 0, tiled=True, axis_index_groups=plain,
    )

    mine = project(0.0, kv_ahead, kv_back, kv_last, 1)
    low = mine[:, size:].astype(bf16)
    low_q, low_v = low[:, :rank], low[:, rank:]
    extra = jnp.dot(low_v, value_up_weight, preferred_element_type=f32)
    mine = (mine[:, :size] + jnp.where(core == 1, extra, 0.0)).astype(bf16)
    q_rows = behind(q_rows.reshape(members * depth, half), kv_ahead[2], kv_back[2])
    q_ahead, q_back = round_y(q_rows, {3: (mine,)})
    q_last = [
        to_chip(q_ahead[-1][:cut], chips, False),
        to_chip(q_back[-1][cut:], -chips, False),
    ]

    mine = jnp.stack([mine] + [to_chip(mine, d, False) for d in range(1, chips)])
    kv = jnp.stack([mine, to_chip(mine, 0, True)])

    up_mine = lax.dynamic_slice_in_dim(query_up_weight, core * half, half, axis=1)
    query = jnp.dot(low_q, up_mine, preferred_element_type=f32)
    query = project(query, q_ahead, q_back, q_last, 0).astype(bf16)

    shifts = lax.dynamic_slice_in_dim(head_shifts, core * (heads // 2), heads // 2)
    seen = jnp.where(shifts != 0, lax.rem(chip + chips // 2, chips), chip)
    info = jnp.concatenate([seen, core[None]]).astype(jnp.int32)
    output, grad_query, value_parts = attend(info, query, grad_out, kv)

    attention_mine = half_of(output, core)
    attention_other = to_chip(half_of(output, 1 - core), 0, True)
    attention = jnp.concatenate(
        [
            jnp.where(core == 0, attention_mine, attention_other),
            jnp.where(core == 0, attention_other, attention_mine),
        ],
        axis=1,
    )

    value_parts = value_parts.reshape(chips, 2, rows, size).astype(bf16)
    same = lax.dynamic_index_in_dim(value_parts, core, 1, keepdims=False)
    cross = lax.dynamic_index_in_dim(value_parts, 1 - core, 1, keepdims=False)
    value_parts = same.astype(f32) + to_chip(cross, 0, True).astype(f32)
    arrived = [value_parts[0]]
    arrived += [to_chip(value_parts[d].astype(bf16), -d, False) for d in range(1, chips)]
    value_gradient = functools.reduce(jnp.add, [a.astype(f32) for a in arrived]).astype(bf16)

    query_up_part = lax.dot_general(low_q, grad_query, TN, preferred_element_type=f32)
    query_up_part = behind(query_up_part.astype(bf16), value_parts)
    query_up_part = query_up_part.reshape(planes, rank // planes, half)
    query_up_part = lax.all_to_all(
        query_up_part, "ctx", 0, 0, tiled=True, axis_index_groups=across
    )
    query_up_part = jnp.sum(
        query_up_part.reshape(planes, rank // planes, half).astype(f32), axis=0
    ).astype(bf16)

    rank_q = lax.dot_general(grad_query, up_mine, NT, preferred_element_type=f32)
    rank_q = half_of(rank_q, core) + to_chip(half_of(rank_q, 1 - core), 0, True)
    rank_v = lax.dot_general(value_gradient, value_up_weight, NT, preferred_element_type=f32)
    rank_terms = jnp.concatenate([rank_q, rank_v], axis=1).astype(bf16)
    rank_grad = jnp.sum(spread(rank_terms, "fsdp").astype(f32), axis=0).astype(bf16)
    grad_down = lax.dot_general(rank_grad, tokens, TN, preferred_element_type=f32)
    grad_down = grad_down.astype(bf16).reshape(2 * rank, devices, depth).transpose(1, 0, 2)
    value_up_part = lax.dot_general(
        half_of(low_v, core), value_gradient, TN, preferred_element_type=f32
    ).astype(bf16)
    shared = jnp.concatenate(
        [value_up_part, query_up_part.reshape(-1, size)], axis=0
    )
    payload = jnp.concatenate(
        [grad_down, jnp.broadcast_to(shared[None], (devices, *shared.shape))], axis=1
    )
    payload = lax.all_to_all(payload, "ctx", 0, 0, tiled=True)
    summed = jnp.sum(payload[:, : 3 * rank].astype(f32), axis=0)
    query_up = payload[:, 3 * rank :].astype(f32)
    query_up = query_up.reshape(planes, chips, 2, rank // planes, half).sum(axis=1)
    query_up_gradient = query_up.transpose(0, 2, 1, 3).reshape(rank, width)
    return (
        attention,
        value_gradient,
        summed[: 2 * rank].T,
        query_up_gradient,
        summed[2 * rank :],
    )


def solution(mesh):
    in_specs = (
        P("ctx", None),
        P("ctx", "fsdp"),
        P("ctx", "fsdp"),
        P("ctx", "fsdp"),
        P("ctx", None),
        P(None, "fsdp"),
        P(None, "fsdp"),
        P("fsdp"),
        P("ctx", "fsdp"),
    )
    out_specs = (
        P("ctx", "fsdp"),
        P("ctx", "fsdp"),
        P("ctx", None),
        P(None, "fsdp"),
        P(None, "fsdp"),
    )
    return jax.shard_map(
        on_device, mesh=mesh, in_specs=in_specs, out_specs=out_specs, check_vma=False
    )
```

```python
import functools

import jax
import jax.numpy as jnp
from jax import lax
from jax.experimental import pallas as pl
from jax.experimental.pallas import tpu as pltpu
from jax.sharding import PartitionSpec as P

GROUP = 2048
bf16 = jnp.bfloat16
f32 = jnp.float32
NT = (((1,), (1,)), ((), ()))
TN = (((0,), (0,)), ((), ()))


def spread(value, axis, groups=None):
    count = len(groups[0]) if groups else lax.axis_size(axis)
    copies = jnp.broadcast_to(value[None], (count, *value.shape))
    return lax.all_to_all(copies, axis, 0, 0, tiled=True, axis_index_groups=groups)


def to_chip(value, chips, other_core):
    count = lax.axis_size("ctx")
    pairs = []
    for source in range(count):
        core = source % 2
        target = (source - core + 2 * chips) % count + (1 - core if other_core else core)
        pairs.append((source, target))
    return lax.ppermute(value, "ctx", pairs)


def attention_kernel(
    scale, tile, info, tokens, weight, start, grad_out, kv,
    out, grad_query, grad_value, query, parts, arrivals,
):
    rows, size = query.shape[0], kv.shape[-1]
    heads = query.shape[1] // size
    blocks, block = kv.shape[1:3]
    keys = [kv.at[info[heads], d] for d in range(blocks)]
    values = [kv.at[1 - info[heads], d] for d in range(blocks)]
    count, depth = parts.shape[:2]
    copies = [
        pltpu.make_async_copy(weight.at[pl.ds(i * depth, depth)], parts.at[i], arrivals.at[i])
        for i in range(count)
    ]
    for copy in copies:
        copy.start()
    grad_value[...] = jnp.zeros_like(grad_value)
    total = start[...]
    for i, copy in enumerate(copies):
        copy.wait()
        part = tokens[:, i * depth : (i + 1) * depth]
        total = total + jnp.dot(part, parts[i], preferred_element_type=f32)
    query[...] = total.astype(bf16)

    def tile_of(index, columns, count):
        here = pl.ds(pl.multiple_of(index * tile, tile), tile)
        q = query[here, columns]
        do = grad_out[here, columns]
        row = index * tile + lax.broadcasted_iota(jnp.int32, (tile, block), 0)
        column = lax.broadcasted_iota(jnp.int32, (tile, block), 1)
        scores = [
            lax.dot_general(q, keys[d][...], NT, preferred_element_type=f32) * scale
            for d in range(count)
        ]
        scores[0] = jnp.where(column <= row, scores[0], -1e30)
        highest = functools.reduce(
            jnp.maximum, [jnp.max(s, axis=1, keepdims=True) for s in scores]
        )
        weights = [jnp.exp(s - highest) for s in scores]
        inverse = 1.0 / functools.reduce(
            jnp.add, [jnp.sum(w, axis=1, keepdims=True) for w in weights]
        )
        probs = [w * inverse for w in weights]
        low = [p.astype(bf16) for p in probs]
        result = functools.reduce(
            jnp.add,
            [
                jnp.dot(low[d], values[d][...], preferred_element_type=f32)
                for d in range(count)
            ],
        ).astype(bf16)
        out[here, columns] = result
        correction = jnp.sum(do.astype(f32) * result.astype(f32), axis=1, keepdims=True)
        total = jnp.zeros((tile, size), f32)
        for d in range(count):
            grad_value[d] += lax.dot_general(low[d], do, TN, preferred_element_type=f32)
            grad_probs = lax.dot_general(do, values[d][...], NT, preferred_element_type=f32)
            grad_scores = (probs[d] * (grad_probs - correction)).astype(bf16)
            total = total + jnp.dot(grad_scores, keys[d][...], preferred_element_type=f32)
        grad_query[here, columns] = (total * scale).astype(bf16)

    for head in range(heads):
        columns = slice(head * size, (head + 1) * size)
        for count in range(1, blocks + 1):

            @pl.when(info[head] + 1 == count)
            def _(columns=columns, count=count):
                def step(index, carry):
                    tile_of(index, columns, count)
                    return carry

                lax.fori_loop(0, rows // tile, step, 0)


def attend(info, tokens, weight, start, grad_out, kv, tile=256, parts=8):
    rows, width = start.shape
    model = tokens.shape[1]
    size = kv.shape[-1]
    blocks, block = kv.shape[1:3]
    vmem = pl.BlockSpec(memory_space=pltpu.VMEM)
    return pl.pallas_call(
        functools.partial(attention_kernel, size ** (-0.5), tile),
        out_shape=(
            jax.ShapeDtypeStruct((rows, width), bf16),
            jax.ShapeDtypeStruct((rows, width), bf16),
            jax.ShapeDtypeStruct((blocks, block, size), f32),
        ),
        in_specs=[
            pl.BlockSpec(memory_space=pltpu.SMEM),
            vmem,
            pl.BlockSpec(memory_space=pl.ANY),
            vmem,
            vmem,
            vmem,
        ],
        out_specs=(vmem, vmem, vmem),
        scratch_shapes=[
            pltpu.VMEM((rows, width), bf16),
            pltpu.VMEM((parts, model // parts, width), bf16),
            pltpu.SemaphoreType.DMA((parts,)),
        ],
        compiler_params=pltpu.CompilerParams(vmem_limit_bytes=48 * 1024 * 1024),
        cost_estimate=pl.CostEstimate(
            flops=10 * rows * width * blocks * block + 2 * rows * width * model,
            bytes_accessed=16 * 1024 * 1024,
            transcendentals=rows * width // size * blocks * block,
        ),
        name="attention",
    )(info, tokens, weight, start, grad_out, kv)


def blocks_kernel(rank_terms, tokens, shared, out):
    ranks, size = rank_terms.shape[0], out.shape[2]
    product = jnp.dot(rank_terms[...], tokens[...], preferred_element_type=f32).astype(bf16)
    for i in range(out.shape[0]):
        out[i, :ranks] = product[:, i * size : (i + 1) * size]
        if out.shape[1] > ranks:
            out[i, ranks:] = shared[...]


def down_blocks(rank_terms, tokens, devices, shared=None, steps=8):
    ranks, rows = rank_terms.shape
    size = tokens.shape[1] // devices
    extra = 0 if shared is None else shared.shape[0]
    if shared is None:
        shared = rank_terms
    step = devices // steps
    return pl.pallas_call(
        blocks_kernel,
        out_shape=jax.ShapeDtypeStruct((devices, ranks + extra, size), bf16),
        grid=(steps,),
        in_specs=[
            pl.BlockSpec((ranks, rows), lambda i: (0, 0)),
            pl.BlockSpec((rows, step * size), lambda i: (0, i)),
            pl.BlockSpec(shared.shape, lambda i: (0, 0)),
        ],
        out_specs=pl.BlockSpec((step, ranks + extra, size), lambda i: (i, 0, 0)),
        compiler_params=pltpu.CompilerParams(vmem_limit_bytes=24 * 1024 * 1024),
        cost_estimate=pl.CostEstimate(
            flops=2 * ranks * rows * devices * size,
            bytes_accessed=2 * rows * devices * size,
            transcendentals=0,
        ),
        name="down_blocks",
    )(rank_terms, tokens, shared)


def on_device(
    tokens,
    query_weight,
    key_weight,
    value_weight,
    adapter_down_weight,
    query_up_weight,
    value_up_weight,
    head_shifts,
    output_gradient,
):
    rows, model = tokens.shape
    heads = head_shifts.shape[0]
    width = query_weight.shape[1]
    size = width // heads
    half = width // 2
    depth = query_weight.shape[0]
    rank = adapter_down_weight.shape[1] // 2
    devices = lax.axis_size("ctx")
    chips = GROUP // (2 * rows)
    members = 2 * chips
    position = lax.axis_index("ctx")
    core = lax.rem(position, 2)
    chip = lax.rem(lax.div(position, 2), chips)
    plain = [[start + i for i in range(members)] for start in range(0, devices, members)]
    across = [[g[i] for g in plain] for i in range(members)]
    planes = devices // members

    def both(mine, theirs):
        return jnp.concatenate(
            [jnp.where(core == 0, mine, theirs), jnp.where(core == 0, theirs, mine)], axis=0
        )

    def half_of(array, which):
        return lax.dynamic_slice_in_dim(array, which * (array.shape[0] // 2), array.shape[0] // 2)

    chip_tokens = both(tokens, to_chip(tokens, 0, True))
    grad_halves = output_gradient.reshape(rows, 2, half).transpose(1, 0, 2)
    grad_mine = lax.dynamic_index_in_dim(grad_halves, core, 0, keepdims=False)
    grad_away = lax.dynamic_index_in_dim(grad_halves, 1 - core, 0, keepdims=False)
    grad_out = both(grad_mine, to_chip(grad_away, 0, True))

    down = adapter_down_weight.T
    kv_rows = jnp.stack(
        [jnp.concatenate([key_weight.T, down]), jnp.concatenate([value_weight.T, down])]
    )
    kv_rows = jnp.broadcast_to(kv_rows[None], (chips, *kv_rows.shape))
    kv_rows = lax.all_to_all(
        kv_rows.reshape(members, size + 2 * rank, depth),
        "ctx", 0, 0, tiled=True, axis_index_groups=plain,
    )
    kv_rows = lax.all_gather(kv_rows, "ctx", axis=0, tiled=True, axis_index_groups=across)
    q_rows = jnp.stack([query_weight[:, :half], query_weight[:, half:]])
    q_rows = jnp.broadcast_to(q_rows[None], (chips, *q_rows.shape))
    q_rows = lax.all_to_all(
        q_rows.reshape(members, depth, half),
        "ctx", 0, 0, tiled=True, axis_index_groups=plain,
    )
    q_rows = lax.all_gather(
        q_rows.reshape(members * depth, half),
        "ctx", axis=0, tiled=True, axis_index_groups=across,
    )

    kv_weight = kv_rows.transpose(1, 0, 2).reshape(size + 2 * rank, model)
    mine = lax.dot_general(chip_tokens, kv_weight, NT, preferred_element_type=f32)
    low = mine[:, size:].astype(bf16)
    low_q, low_v = low[:, :rank], low[:, rank:]
    extra = jnp.dot(low_v, value_up_weight, preferred_element_type=f32)
    mine = (mine[:, :size] + jnp.where(core == 1, extra, 0.0)).astype(bf16)
    mine = jnp.stack([mine] + [to_chip(mine, d, False) for d in range(1, chips)])
    kv = jnp.stack([mine, to_chip(mine, 0, True)])

    up_mine = lax.dynamic_slice_in_dim(query_up_weight, core * half, half, axis=1)
    start = jnp.dot(low_q, up_mine, preferred_element_type=f32)
    shifts = lax.dynamic_slice_in_dim(head_shifts, core * (heads // 2), heads // 2)
    seen = jnp.where(shifts != 0, lax.rem(chip + chips // 2, chips), chip)
    info = jnp.concatenate([seen, core[None]]).astype(jnp.int32)
    output, grad_query, value_parts = attend(info, chip_tokens, q_rows, start, grad_out, kv)

    attention_mine = half_of(output, core)
    attention_other = to_chip(half_of(output, 1 - core), 0, True)
    attention = jnp.concatenate(
        [
            jnp.where(core == 0, attention_mine, attention_other),
            jnp.where(core == 0, attention_other, attention_mine),
        ],
        axis=1,
    )

    rank_q = lax.dot_general(up_mine, grad_query, NT, preferred_element_type=f32).astype(bf16)
    q_blocks = lax.all_to_all(
        down_blocks(rank_q, chip_tokens, devices), "ctx", 0, 0, tiled=True
    )

    query_up_part = lax.dot_general(low_q, grad_query, TN, preferred_element_type=f32)
    query_up_part = query_up_part.reshape(chips, -1, size)
    value_parts = value_parts.reshape(chips, 2, rows, size).astype(bf16)
    same = lax.dynamic_index_in_dim(value_parts, core, 1, keepdims=False)
    cross = lax.dynamic_index_in_dim(value_parts, 1 - core, 1, keepdims=False)
    value_parts = same.astype(f32) + to_chip(cross, 0, True).astype(f32)

    def with_share(d):
        share = lax.dynamic_index_in_dim(
            query_up_part, lax.rem(chip + chips - d, chips), 0, keepdims=False
        )
        return jnp.concatenate([value_parts[d], share], axis=0)

    arrived = [with_share(0)]
    arrived += [to_chip(with_share(d).astype(bf16), -d, False) for d in range(1, chips)]
    arrived = functools.reduce(jnp.add, [a.astype(f32) for a in arrived]).astype(bf16)
    value_gradient = arrived[:rows]

    rank_v = lax.dot_general(
        value_up_weight, value_gradient, NT, preferred_element_type=f32
    ).astype(bf16)
    value_up_part = lax.dot_general(
        half_of(low_v, core), value_gradient, TN, preferred_element_type=f32
    ).astype(bf16)
    shared = jnp.concatenate([value_up_part, arrived[rows:]], axis=0)
    v_blocks = lax.all_to_all(
        down_blocks(rank_v, tokens, devices, shared), "ctx", 0, 0, tiled=True
    )
    grad_down = jnp.concatenate(
        [
            jnp.sum(q_blocks.astype(f32), axis=0),
            jnp.sum(v_blocks[:, :rank].astype(f32), axis=0),
        ],
        axis=0,
    ).astype(bf16)
    grad_down = jnp.sum(spread(grad_down, "fsdp").astype(f32), axis=0)
    value_up_gradient = jnp.sum(v_blocks[:, rank : 2 * rank].astype(f32), axis=0)
    query_up = v_blocks[:, 2 * rank :].astype(f32)
    query_up = query_up.reshape(planes, chips, 2, rank // chips, half).sum(axis=0)
    query_up_gradient = query_up.transpose(0, 2, 1, 3).reshape(rank, width)
    return (attention, value_gradient, grad_down.T, query_up_gradient, value_up_gradient)


def solution(mesh):
    in_specs = (
        P("ctx", None),
        P("ctx", "fsdp"),
        P("ctx", "fsdp"),
        P("ctx", "fsdp"),
        P("ctx", None),
        P(None, "fsdp"),
        P(None, "fsdp"),
        P("fsdp"),
        P("ctx", "fsdp"),
    )
    out_specs = (
        P("ctx", "fsdp"),
        P("ctx", "fsdp"),
        P("ctx", None),
        P(None, "fsdp"),
        P(None, "fsdp"),
    )
    return jax.shard_map(
        on_device, mesh=mesh, in_specs=in_specs, out_specs=out_specs, check_vma=False
    )
```

```python
import functools

import jax
import jax.numpy as jnp
from jax import lax
from jax.experimental import pallas as pl
from jax.experimental.pallas import tpu as pltpu
from jax.sharding import PartitionSpec as P

GROUP = 2048
bf16 = jnp.bfloat16
f32 = jnp.float32
NT = (((1,), (1,)), ((), ()))
TN = (((0,), (0,)), ((), ()))


def spread(value, axis, groups=None):
    count = len(groups[0]) if groups else lax.axis_size(axis)
    copies = jnp.broadcast_to(value[None], (count, *value.shape))
    return lax.all_to_all(copies, axis, 0, 0, tiled=True, axis_index_groups=groups)


def to_chip(value, chips, other_core):
    count = lax.axis_size("ctx")
    pairs = []
    for source in range(count):
        core = source % 2
        target = (source - core + 2 * chips) % count + (1 - core if other_core else core)
        pairs.append((source, target))
    return lax.ppermute(value, "ctx", pairs)


def attention_kernel(
    scale, tile, info, tokens, weight, start, grad_out, kv,
    out, grad_query, grad_value, query, columns_in, rows_in, arrivals,
):
    rows, size = query.shape[0], kv.shape[-1]
    heads = query.shape[1] // size
    blocks, block = kv.shape[1:3]
    keys = [kv.at[info[heads], d] for d in range(blocks)]
    values = [kv.at[1 - info[heads], d] for d in range(blocks)]
    parts, depth = rows_in.shape[:2]
    copies = []
    for i in range(parts):
        here = pl.ds(i * depth, depth)
        copies += [
            pltpu.make_async_copy(tokens.at[:, here], columns_in.at[i], arrivals.at[2 * i]),
            pltpu.make_async_copy(weight.at[here], rows_in.at[i], arrivals.at[2 * i + 1]),
        ]
    for copy in copies:
        copy.start()
    grad_value[...] = jnp.zeros_like(grad_value)
    total = start[...]
    for i in range(parts):
        copies[2 * i].wait()
        copies[2 * i + 1].wait()
        total = total + jnp.dot(columns_in[i], rows_in[i], preferred_element_type=f32)
    query[...] = total.astype(bf16)

    def tile_of(index, columns, count):
        here = pl.ds(pl.multiple_of(index * tile, tile), tile)
        q = query[here, columns]
        do = grad_out[here, columns]
        row = index * tile + lax.broadcasted_iota(jnp.int32, (tile, block), 0)
        column = lax.broadcasted_iota(jnp.int32, (tile, block), 1)
        scores = [
            lax.dot_general(q, keys[d][...], NT, preferred_element_type=f32) * scale
            for d in range(count)
        ]
        scores[0] = jnp.where(column <= row, scores[0], -1e30)
        highest = functools.reduce(
            jnp.maximum, [jnp.max(s, axis=1, keepdims=True) for s in scores]
        )
        weights = [jnp.exp(s - highest) for s in scores]
        inverse = 1.0 / functools.reduce(
            jnp.add, [jnp.sum(w, axis=1, keepdims=True) for w in weights]
        )
        probs = [w * inverse for w in weights]
        low = [p.astype(bf16) for p in probs]
        result = functools.reduce(
            jnp.add,
            [
                jnp.dot(low[d], values[d][...], preferred_element_type=f32)
                for d in range(count)
            ],
        ).astype(bf16)
        out[here, columns] = result
        correction = jnp.sum(do.astype(f32) * result.astype(f32), axis=1, keepdims=True)
        total = jnp.zeros((tile, size), f32)
        for d in range(count):
            grad_value[d] += lax.dot_general(low[d], do, TN, preferred_element_type=f32)
            grad_probs = lax.dot_general(do, values[d][...], NT, preferred_element_type=f32)
            grad_scores = (probs[d] * (grad_probs - correction)).astype(bf16)
            total = total + jnp.dot(grad_scores, keys[d][...], preferred_element_type=f32)
        grad_query[here, columns] = (total * scale).astype(bf16)

    for head in range(heads):
        columns = slice(head * size, (head + 1) * size)
        for count in range(1, blocks + 1):

            @pl.when(info[head] + 1 == count)
            def _(columns=columns, count=count):
                def step(index, carry):
                    tile_of(index, columns, count)
                    return carry

                lax.fori_loop(0, rows // tile, step, 0)


def attend(info, tokens, weight, start, grad_out, kv, tile=256, parts=8):
    rows, width = start.shape
    model = tokens.shape[1]
    size = kv.shape[-1]
    blocks, block = kv.shape[1:3]
    vmem = pl.BlockSpec(memory_space=pltpu.VMEM)
    return pl.pallas_call(
        functools.partial(attention_kernel, size ** (-0.5), tile),
        out_shape=(
            jax.ShapeDtypeStruct((rows, width), bf16),
            jax.ShapeDtypeStruct((rows, width), bf16),
            jax.ShapeDtypeStruct((blocks, block, size), f32),
        ),
        in_specs=[
            pl.BlockSpec(memory_space=pltpu.SMEM),
            pl.BlockSpec(memory_space=pl.ANY),
            pl.BlockSpec(memory_space=pl.ANY),
            vmem,
            vmem,
            vmem,
        ],
        out_specs=(vmem, vmem, vmem),
        scratch_shapes=[
            pltpu.VMEM((rows, width), bf16),
            pltpu.VMEM((parts, rows, model // parts), bf16),
            pltpu.VMEM((parts, model // parts, width), bf16),
            pltpu.SemaphoreType.DMA((2 * parts,)),
        ],
        compiler_params=pltpu.CompilerParams(vmem_limit_bytes=48 * 1024 * 1024),
        cost_estimate=pl.CostEstimate(
            flops=10 * rows * width * blocks * block + 2 * rows * width * model,
            bytes_accessed=16 * 1024 * 1024,
            transcendentals=rows * width // size * blocks * block,
        ),
        name="attention",
    )(info, tokens, weight, start, grad_out, kv)


def blocks_kernel(rank_terms, tokens, above, below, out):
    top, size = above.shape[1], out.shape[2]
    bottom = top + rank_terms.shape[0]
    product = jnp.dot(rank_terms[...], tokens[...], preferred_element_type=f32).astype(bf16)
    for i in range(out.shape[0]):
        out[i, :top] = above[i]
        out[i, top:bottom] = product[:, i * size : (i + 1) * size]
        out[i, bottom:] = below[...]


def first_blocks_kernel(rank_terms, tokens, out):
    size = out.shape[2]
    product = jnp.dot(rank_terms[...], tokens[...], preferred_element_type=f32).astype(bf16)
    for i in range(out.shape[0]):
        out[i] = product[:, i * size : (i + 1) * size]


def down_blocks(rank_terms, tokens, devices, above=None, below=None, steps=4):
    ranks, rows = rank_terms.shape
    size = tokens.shape[1] // devices
    step = devices // steps
    in_specs = [
        pl.BlockSpec((ranks, rows), lambda i: (0, 0)),
        pl.BlockSpec((rows, step * size), lambda i: (0, i)),
    ]
    more, height, kernel = (), ranks, first_blocks_kernel
    if above is not None:
        more, kernel = (above, below), blocks_kernel
        height += above.shape[1] + below.shape[0]
        in_specs += [
            pl.BlockSpec((step, *above.shape[1:]), lambda i: (i, 0, 0)),
            pl.BlockSpec(below.shape, lambda i: (0, 0)),
        ]
    return pl.pallas_call(
        kernel,
        out_shape=jax.ShapeDtypeStruct((devices, height, size), bf16),
        grid=(steps,),
        in_specs=in_specs,
        out_specs=pl.BlockSpec((step, height, size), lambda i: (i, 0, 0)),
        compiler_params=pltpu.CompilerParams(vmem_limit_bytes=56 * 1024 * 1024),
        cost_estimate=pl.CostEstimate(
            flops=2 * ranks * rows * devices * size,
            bytes_accessed=2 * rows * devices * size,
            transcendentals=0,
        ),
        name="down_blocks",
    )(rank_terms, tokens, *more)


def on_device(
    tokens,
    query_weight,
    key_weight,
    value_weight,
    adapter_down_weight,
    query_up_weight,
    value_up_weight,
    head_shifts,
    output_gradient,
):
    rows, model = tokens.shape
    heads = head_shifts.shape[0]
    width = query_weight.shape[1]
    size = width // heads
    half = width // 2
    depth = query_weight.shape[0]
    rank = adapter_down_weight.shape[1] // 2
    devices = lax.axis_size("ctx")
    chips = GROUP // (2 * rows)
    members = 2 * chips
    position = lax.axis_index("ctx")
    core = lax.rem(position, 2)
    chip = lax.rem(lax.div(position, 2), chips)
    plain = [[start + i for i in range(members)] for start in range(0, devices, members)]
    across = [[g[i] for g in plain] for i in range(members)]
    planes = devices // members

    def both(mine, theirs):
        return jnp.concatenate(
            [jnp.where(core == 0, mine, theirs), jnp.where(core == 0, theirs, mine)], axis=0
        )

    def half_of(array, which):
        return lax.dynamic_slice_in_dim(array, which * (array.shape[0] // 2), array.shape[0] // 2)

    chip_tokens = both(tokens, to_chip(tokens, 0, True))
    grad_halves = output_gradient.reshape(rows, 2, half).transpose(1, 0, 2)
    grad_mine = lax.dynamic_index_in_dim(grad_halves, core, 0, keepdims=False)
    grad_away = lax.dynamic_index_in_dim(grad_halves, 1 - core, 0, keepdims=False)
    grad_out = both(grad_mine, to_chip(grad_away, 0, True))

    down = adapter_down_weight.T
    kv_rows = jnp.stack(
        [jnp.concatenate([key_weight.T, down]), jnp.concatenate([value_weight.T, down])]
    )
    kv_rows = jnp.broadcast_to(kv_rows[None], (chips, *kv_rows.shape))
    kv_rows = lax.all_to_all(
        kv_rows.reshape(members, size + 2 * rank, depth),
        "ctx", 0, 0, tiled=True, axis_index_groups=plain,
    )
    kv_rows = lax.all_gather(kv_rows, "ctx", axis=0, tiled=True, axis_index_groups=across)
    q_rows = jnp.stack([query_weight[:, :half], query_weight[:, half:]])
    q_rows = jnp.broadcast_to(q_rows[None], (chips, *q_rows.shape))
    q_rows = lax.all_to_all(
        q_rows.reshape(members, depth, half),
        "ctx", 0, 0, tiled=True, axis_index_groups=plain,
    )
    q_rows = lax.all_gather(
        q_rows.reshape(members * depth, half),
        "ctx", axis=0, tiled=True, axis_index_groups=across,
    )

    kv_weight = kv_rows.transpose(1, 0, 2).reshape(size + 2 * rank, model)
    mine = lax.dot_general(chip_tokens, kv_weight, NT, preferred_element_type=f32)
    low = mine[:, size:].astype(bf16)
    low_q, low_v = low[:, :rank], low[:, rank:]
    extra = jnp.dot(low_v, value_up_weight, preferred_element_type=f32)
    mine = (mine[:, :size] + jnp.where(core == 1, extra, 0.0)).astype(bf16)
    mine = jnp.stack([mine] + [to_chip(mine, d, False) for d in range(1, chips)])
    kv = jnp.stack([mine, to_chip(mine, 0, True)])

    up_mine = lax.dynamic_slice_in_dim(query_up_weight, core * half, half, axis=1)
    start = jnp.dot(low_q, up_mine, preferred_element_type=f32)
    shifts = lax.dynamic_slice_in_dim(head_shifts, core * (heads // 2), heads // 2)
    seen = jnp.where(shifts != 0, lax.rem(chip + chips // 2, chips), chip)
    info = jnp.concatenate([seen, core[None]]).astype(jnp.int32)
    output, grad_query, value_parts = attend(info, chip_tokens, q_rows, start, grad_out, kv)

    attention_mine = half_of(output, core)
    attention_other = to_chip(half_of(output, 1 - core), 0, True)
    attention = jnp.concatenate(
        [
            jnp.where(core == 0, attention_mine, attention_other),
            jnp.where(core == 0, attention_other, attention_mine),
        ],
        axis=1,
    )

    rank_q = lax.dot_general(up_mine, grad_query, NT, preferred_element_type=f32).astype(bf16)
    q_blocks = down_blocks(rank_q, chip_tokens, devices)

    query_up_part = lax.dot_general(low_q, grad_query, TN, preferred_element_type=f32)
    query_up_part = query_up_part.reshape(chips, -1, size)
    value_parts = value_parts.reshape(chips, 2, rows, size).astype(bf16)
    same = lax.dynamic_index_in_dim(value_parts, core, 1, keepdims=False)
    cross = lax.dynamic_index_in_dim(value_parts, 1 - core, 1, keepdims=False)
    value_parts = same.astype(f32) + to_chip(cross, 0, True).astype(f32)

    def with_share(d):
        share = lax.dynamic_index_in_dim(
            query_up_part, lax.rem(chip + chips - d, chips), 0, keepdims=False
        )
        return jnp.concatenate([value_parts[d], share], axis=0)

    arrived = [with_share(0)]
    arrived += [to_chip(with_share(d).astype(bf16), -d, False) for d in range(1, chips)]
    arrived = functools.reduce(jnp.add, [a.astype(f32) for a in arrived]).astype(bf16)
    value_gradient = arrived[:rows]

    rank_v = lax.dot_general(
        value_up_weight, value_gradient, NT, preferred_element_type=f32
    ).astype(bf16)
    value_up_part = lax.dot_general(
        half_of(low_v, core), value_gradient, TN, preferred_element_type=f32
    ).astype(bf16)
    shared = jnp.concatenate([value_up_part, arrived[rows:]], axis=0)
    blocks = down_blocks(rank_v, tokens, devices, q_blocks, shared)
    blocks = lax.all_to_all(blocks, "ctx", 0, 0, tiled=True)
    summed = jnp.sum(blocks[:, : 3 * rank].astype(f32), axis=0)
    grad_down = jnp.sum(spread(summed[: 2 * rank].astype(bf16), "fsdp").astype(f32), axis=0)
    value_up_gradient = summed[2 * rank :]
    query_up = blocks[:, 3 * rank :].astype(f32)
    query_up = query_up.reshape(planes, chips, 2, rank // chips, half).sum(axis=0)
    query_up_gradient = query_up.transpose(0, 2, 1, 3).reshape(rank, width)
    return (attention, value_gradient, grad_down.T, query_up_gradient, value_up_gradient)


def solution(mesh):
    in_specs = (
        P("ctx", None),
        P("ctx", "fsdp"),
        P("ctx", "fsdp"),
        P("ctx", "fsdp"),
        P("ctx", None),
        P(None, "fsdp"),
        P(None, "fsdp"),
        P("fsdp"),
        P("ctx", "fsdp"),
    )
    out_specs = (
        P("ctx", "fsdp"),
        P("ctx", "fsdp"),
        P("ctx", None),
        P(None, "fsdp"),
        P(None, "fsdp"),
    )
    return jax.shard_map(
        on_device, mesh=mesh, in_specs=in_specs, out_specs=out_specs, check_vma=False
    )
```

```python
import functools

import jax
import jax.numpy as jnp
from jax import lax
from jax.experimental import pallas as pl
from jax.experimental.pallas import tpu as pltpu
from jax.sharding import PartitionSpec as P

GROUP = 2048
bf16 = jnp.bfloat16
f32 = jnp.float32
NT = (((1,), (1,)), ((), ()))
TN = (((0,), (0,)), ((), ()))


def spread(value, axis, groups=None):
    count = len(groups[0]) if groups else lax.axis_size(axis)
    copies = jnp.broadcast_to(value[None], (count, *value.shape))
    return lax.all_to_all(copies, axis, 0, 0, tiled=True, axis_index_groups=groups)


def to_chip(value, chips, other_core):
    count = lax.axis_size("ctx")
    pairs = []
    for source in range(count):
        core = source % 2
        target = (source - core + 2 * chips) % count + (1 - core if other_core else core)
        pairs.append((source, target))
    return lax.ppermute(value, "ctx", pairs)


def rows_of(tokens, theirs, columns, core, target, arrivals, first):
    rows = tokens.shape[0]
    mine = target.at[pl.ds(pl.multiple_of(core * rows, rows), rows)]
    other = target.at[pl.ds(pl.multiple_of((1 - core) * rows, rows), rows)]
    return [
        pltpu.make_async_copy(tokens.at[:, columns], mine, arrivals.at[first]),
        pltpu.make_async_copy(theirs.at[:, columns], other, arrivals.at[first + 1]),
    ]


def project_kernel(steps, info, tokens, theirs, up, *rest):
    chunks, (out, low_out, columns_in, arrivals) = rest[: len(steps)], rest[len(steps) :]
    planes, _, depth = columns_in.shape
    size = out.shape[1]
    plane, core = info[0], info[1]
    copies = []
    for i in range(planes):
        start = lax.rem(plane + i, planes) * depth
        here = pl.ds(pl.multiple_of(start, depth), depth)
        copies.append(rows_of(tokens, theirs, here, core, columns_in.at[i], arrivals, 2 * i))
    order = list(dict.fromkeys(step for step, _ in steps))
    for step in order:
        for copy in copies[step]:
            copy.start()
    total = jnp.zeros((out.shape[0], chunks[0].shape[0]), f32)
    waited = set()
    for (step, place), chunk in zip(steps, chunks):
        if step not in waited:
            waited.add(step)
            for copy in copies[step]:
                copy.wait()
        part = columns_in[step, :, place : place + chunk.shape[1]]
        total = total + lax.dot_general(part, chunk[...], NT, preferred_element_type=f32)
    low = total[:, size:].astype(bf16)
    low_out[...] = low
    rank = low.shape[1] // 2
    extra = jnp.dot(low[:, rank:], up[...], preferred_element_type=f32)
    out[...] = (total[:, :size] + jnp.where(core == 1, extra, 0.0)).astype(bf16)


def project(info, tokens, theirs, up, steps, chunks, planes):
    rows, model = tokens.shape
    size = up.shape[1]
    ranks = chunks[0].shape[0] - size
    vmem = pl.BlockSpec(memory_space=pltpu.VMEM)
    anywhere = pl.BlockSpec(memory_space=pl.ANY)
    return pl.pallas_call(
        functools.partial(project_kernel, steps),
        out_shape=(
            jax.ShapeDtypeStruct((2 * rows, size), bf16),
            jax.ShapeDtypeStruct((2 * rows, ranks), bf16),
        ),
        in_specs=[pl.BlockSpec(memory_space=pltpu.SMEM), anywhere, anywhere, vmem]
        + [vmem] * len(chunks),
        out_specs=(vmem, vmem),
        scratch_shapes=[
            pltpu.VMEM((planes, 2 * rows, model // planes), bf16),
            pltpu.SemaphoreType.DMA((2 * planes,)),
        ],
        compiler_params=pltpu.CompilerParams(vmem_limit_bytes=48 * 1024 * 1024),
        cost_estimate=pl.CostEstimate(
            flops=4 * rows * model * (size + ranks),
            bytes_accessed=4 * rows * model,
            transcendentals=0,
        ),
        name="project",
    )(info, tokens, theirs, up, *chunks)


def attention_kernel(
    scale, tile, info, tokens, theirs, weight, start, grad_out, kv,
    out, grad_query, grad_value, query, columns_in, rows_in, arrivals,
):
    rows, size = query.shape[0], kv.shape[-1]
    heads = query.shape[1] // size
    blocks, block = kv.shape[1:3]
    keys = [kv.at[info[heads], d] for d in range(blocks)]
    values = [kv.at[1 - info[heads], d] for d in range(blocks)]
    parts, depth = rows_in.shape[:2]
    copies = []
    for i in range(parts):
        here = pl.ds(i * depth, depth)
        copies.append(
            rows_of(tokens, theirs, here, info[heads], columns_in.at[i], arrivals, 3 * i)
            + [pltpu.make_async_copy(weight.at[here], rows_in.at[i], arrivals.at[3 * i + 2])]
        )
    for copy in sum(copies, []):
        copy.start()
    grad_value[...] = jnp.zeros_like(grad_value)
    total = start[...]
    for i in range(parts):
        for copy in copies[i]:
            copy.wait()
        total = total + jnp.dot(columns_in[i], rows_in[i], preferred_element_type=f32)
    query[...] = total.astype(bf16)

    def tile_of(index, columns, count):
        here = pl.ds(pl.multiple_of(index * tile, tile), tile)
        q = query[here, columns]
        do = grad_out[here, columns]
        row = index * tile + lax.broadcasted_iota(jnp.int32, (tile, block), 0)
        column = lax.broadcasted_iota(jnp.int32, (tile, block), 1)
        scores = [
            lax.dot_general(q, keys[d][...], NT, preferred_element_type=f32) * scale
            for d in range(count)
        ]
        scores[0] = jnp.where(column <= row, scores[0], -1e30)
        highest = functools.reduce(
            jnp.maximum, [jnp.max(s, axis=1, keepdims=True) for s in scores]
        )
        weights = [jnp.exp(s - highest) for s in scores]
        inverse = 1.0 / functools.reduce(
            jnp.add, [jnp.sum(w, axis=1, keepdims=True) for w in weights]
        )
        probs = [w * inverse for w in weights]
        low = [p.astype(bf16) for p in probs]
        result = functools.reduce(
            jnp.add,
            [
                jnp.dot(low[d], values[d][...], preferred_element_type=f32)
                for d in range(count)
            ],
        ).astype(bf16)
        out[here, columns] = result
        correction = jnp.sum(do.astype(f32) * result.astype(f32), axis=1, keepdims=True)
        total = jnp.zeros((tile, size), f32)
        for d in range(count):
            grad_value[d] += lax.dot_general(low[d], do, TN, preferred_element_type=f32)
            grad_probs = lax.dot_general(do, values[d][...], NT, preferred_element_type=f32)
            grad_scores = (probs[d] * (grad_probs - correction)).astype(bf16)
            total = total + jnp.dot(grad_scores, keys[d][...], preferred_element_type=f32)
        grad_query[here, columns] = (total * scale).astype(bf16)

    for head in range(heads):
        columns = slice(head * size, (head + 1) * size)
        for count in range(1, blocks + 1):

            @pl.when(info[head] + 1 == count)
            def _(columns=columns, count=count):
                def step(index, carry):
                    tile_of(index, columns, count)
                    return carry

                lax.fori_loop(0, rows // tile, step, 0)


def attend(info, tokens, theirs, weight, start, grad_out, kv, tile=256, parts=8):
    rows, width = start.shape
    model = tokens.shape[1]
    size = kv.shape[-1]
    blocks, block = kv.shape[1:3]
    vmem = pl.BlockSpec(memory_space=pltpu.VMEM)
    return pl.pallas_call(
        functools.partial(attention_kernel, size ** (-0.5), tile),
        out_shape=(
            jax.ShapeDtypeStruct((rows, width), bf16),
            jax.ShapeDtypeStruct((rows, width), bf16),
            jax.ShapeDtypeStruct((blocks, block, size), f32),
        ),
        in_specs=[
            pl.BlockSpec(memory_space=pltpu.SMEM),
            pl.BlockSpec(memory_space=pl.ANY),
            pl.BlockSpec(memory_space=pl.ANY),
            pl.BlockSpec(memory_space=pl.ANY),
            vmem,
            vmem,
            vmem,
        ],
        out_specs=(vmem, vmem, vmem),
        scratch_shapes=[
            pltpu.VMEM((rows, width), bf16),
            pltpu.VMEM((parts, rows, model // parts), bf16),
            pltpu.VMEM((parts, model // parts, width), bf16),
            pltpu.SemaphoreType.DMA((3 * parts,)),
        ],
        compiler_params=pltpu.CompilerParams(vmem_limit_bytes=48 * 1024 * 1024),
        cost_estimate=pl.CostEstimate(
            flops=10 * rows * width * blocks * block + 2 * rows * width * model,
            bytes_accessed=16 * 1024 * 1024,
            transcendentals=rows * width // size * blocks * block,
        ),
        name="attention",
    )(info, tokens, theirs, weight, start, grad_out, kv)


def blocks_kernel(rank_terms, tokens, above, below, out):
    top, size = above.shape[1], out.shape[2]
    bottom = top + rank_terms.shape[0]
    product = jnp.dot(rank_terms[...], tokens[...], preferred_element_type=f32).astype(bf16)
    for i in range(out.shape[0]):
        out[i, :top] = above[i]
        out[i, top:bottom] = product[:, i * size : (i + 1) * size]
        out[i, bottom:] = below[...]


def first_blocks_kernel(rank_mine, rank_theirs, tokens, theirs, out):
    size = out.shape[2]
    product = jnp.dot(rank_mine[...], tokens[...], preferred_element_type=f32)
    product += jnp.dot(rank_theirs[...], theirs[...], preferred_element_type=f32)
    product = product.astype(bf16)
    for i in range(out.shape[0]):
        out[i] = product[:, i * size : (i + 1) * size]


def down_blocks(kernel, ranks, tokens, devices, above=None, below=None, steps=8):
    rows, model = tokens[0].shape
    size = model // devices
    step = devices // steps
    height = ranks[0].shape[0]
    in_specs = [pl.BlockSpec(r.shape, lambda i: (0, 0)) for r in ranks]
    in_specs += [pl.BlockSpec((rows, step * size), lambda i: (0, i)) for _ in tokens]
    more = ()
    if above is not None:
        more = (above, below)
        height += above.shape[1] + below.shape[0]
        in_specs += [
            pl.BlockSpec((step, *above.shape[1:]), lambda i: (i, 0, 0)),
            pl.BlockSpec(below.shape, lambda i: (0, 0)),
        ]
    return pl.pallas_call(
        kernel,
        out_shape=jax.ShapeDtypeStruct((devices, height, size), bf16),
        grid=(steps,),
        in_specs=in_specs,
        out_specs=pl.BlockSpec((step, height, size), lambda i: (i, 0, 0)),
        compiler_params=pltpu.CompilerParams(vmem_limit_bytes=56 * 1024 * 1024),
        cost_estimate=pl.CostEstimate(
            flops=2 * ranks[0].shape[0] * rows * model * len(tokens),
            bytes_accessed=2 * rows * model * len(tokens),
            transcendentals=0,
        ),
        name="down_blocks",
    )(*ranks, *tokens, *more)


def on_device(
    tokens,
    query_weight,
    key_weight,
    value_weight,
    adapter_down_weight,
    query_up_weight,
    value_up_weight,
    head_shifts,
    output_gradient,
):
    rows, model = tokens.shape
    heads = head_shifts.shape[0]
    width = query_weight.shape[1]
    size = width // heads
    half = width // 2
    depth = query_weight.shape[0]
    rank = adapter_down_weight.shape[1] // 2
    devices = lax.axis_size("ctx")
    chips = GROUP // (2 * rows)
    members = 2 * chips
    position = lax.axis_index("ctx")
    core = lax.rem(position, 2)
    chip = lax.rem(lax.div(position, 2), chips)
    plain = [[start + i for i in range(members)] for start in range(0, devices, members)]
    across = [[g[i] for g in plain] for i in range(members)]
    planes = devices // members

    def both(mine, theirs):
        return jnp.concatenate(
            [jnp.where(core == 0, mine, theirs), jnp.where(core == 0, theirs, mine)], axis=0
        )

    def half_of(array, which):
        return lax.dynamic_slice_in_dim(array, which * (array.shape[0] // 2), array.shape[0] // 2)

    def round_y(value):
        ahead, back = [value], [value]
        for _ in range(planes // 2 - 1):
            ahead.append(to_chip(ahead[-1], chips, False))
            back.append(to_chip(back[-1], -chips, False))
        return ahead, back

    def behind(value, earlier):
        return value + (earlier.reshape(-1)[0] * 0).astype(value.dtype)

    theirs = to_chip(tokens, 0, True)
    grad_halves = output_gradient.reshape(rows, 2, half).transpose(1, 0, 2)
    grad_mine = lax.dynamic_index_in_dim(grad_halves, core, 0, keepdims=False)
    grad_away = lax.dynamic_index_in_dim(grad_halves, 1 - core, 0, keepdims=False)
    grad_out = both(grad_mine, to_chip(grad_away, 0, True))

    down = adapter_down_weight.T
    kv_rows = jnp.stack(
        [jnp.concatenate([key_weight.T, down]), jnp.concatenate([value_weight.T, down])]
    )
    kv_rows = jnp.broadcast_to(kv_rows[None], (chips, *kv_rows.shape))
    kv_rows = lax.all_to_all(
        kv_rows.reshape(members, size + 2 * rank, depth),
        "ctx", 0, 0, tiled=True, axis_index_groups=plain,
    )
    kv_rows = kv_rows.transpose(1, 0, 2).reshape(size + 2 * rank, members * depth)
    kv_ahead, kv_back = round_y(kv_rows)
    cut = members * depth // 2
    opposite = planes // 2
    steps, chunks = [(0, 0)], [kv_rows]
    for step in range(1, opposite):
        steps += [(planes - step, 0), (step, 0)]
        chunks += [kv_ahead[step], kv_back[step]]
    steps += [(opposite, 0), (opposite, cut)]
    chunks += [
        to_chip(kv_ahead[-1][:, :cut], chips, False),
        to_chip(kv_back[-1][:, cut:], -chips, False),
    ]
    q_rows = behind(jnp.stack([query_weight[:, :half], query_weight[:, half:]]), kv_rows)
    q_rows = jnp.broadcast_to(q_rows[None], (chips, *q_rows.shape))
    q_rows = lax.all_to_all(
        q_rows.reshape(members, depth, half),
        "ctx", 0, 0, tiled=True, axis_index_groups=plain,
    )
    q_rows = lax.all_gather(
        q_rows.reshape(members * depth, half),
        "ctx", axis=0, tiled=True, axis_index_groups=across,
    )

    place = jnp.stack([lax.div(position, members), core]).astype(jnp.int32)
    mine, low = project(place, tokens, theirs, value_up_weight, steps, chunks, planes)
    low_q, low_v = low[:, :rank], low[:, rank:]
    mine = jnp.stack([mine] + [to_chip(mine, d, False) for d in range(1, chips)])
    kv = jnp.stack([mine, to_chip(mine, 0, True)])

    up_mine = lax.dynamic_slice_in_dim(query_up_weight, core * half, half, axis=1)
    start = jnp.dot(low_q, up_mine, preferred_element_type=f32)
    shifts = lax.dynamic_slice_in_dim(head_shifts, core * (heads // 2), heads // 2)
    seen = jnp.where(shifts != 0, lax.rem(chip + chips // 2, chips), chip)
    info = jnp.concatenate([seen, core[None]]).astype(jnp.int32)
    output, grad_query, value_parts = attend(
        info, tokens, theirs, q_rows, start, grad_out, kv
    )

    attention_mine = half_of(output, core)
    attention_other = to_chip(half_of(output, 1 - core), 0, True)
    attention = jnp.concatenate(
        [
            jnp.where(core == 0, attention_mine, attention_other),
            jnp.where(core == 0, attention_other, attention_mine),
        ],
        axis=1,
    )

    rank_q = lax.dot_general(up_mine, grad_query, NT, preferred_element_type=f32).astype(bf16)
    rank_halves = rank_q.reshape(rank, 2, rows)
    rank_mine = lax.dynamic_index_in_dim(rank_halves, core, 1, keepdims=False)
    rank_theirs = lax.dynamic_index_in_dim(rank_halves, 1 - core, 1, keepdims=False)
    q_blocks = down_blocks(
        first_blocks_kernel, (rank_mine, rank_theirs), (tokens, theirs), devices
    )

    query_up_part = lax.dot_general(low_q, grad_query, TN, preferred_element_type=f32)
    query_up_part = query_up_part.reshape(chips, -1, size)
    value_parts = value_parts.reshape(chips, 2, rows, size).astype(bf16)
    same = lax.dynamic_index_in_dim(value_parts, core, 1, keepdims=False)
    cross = lax.dynamic_index_in_dim(value_parts, 1 - core, 1, keepdims=False)
    value_parts = same.astype(f32) + to_chip(cross, 0, True).astype(f32)

    def with_share(d):
        share = lax.dynamic_index_in_dim(
            query_up_part, lax.rem(chip + chips - d, chips), 0, keepdims=False
        )
        return jnp.concatenate([value_parts[d], share], axis=0)

    arrived = [with_share(0)]
    arrived += [to_chip(with_share(d).astype(bf16), -d, False) for d in range(1, chips)]
    arrived = functools.reduce(jnp.add, [a.astype(f32) for a in arrived]).astype(bf16)
    value_gradient = arrived[:rows]

    rank_v = lax.dot_general(
        value_up_weight, value_gradient, NT, preferred_element_type=f32
    ).astype(bf16)
    value_up_part = lax.dot_general(
        half_of(low_v, core), value_gradient, TN, preferred_element_type=f32
    ).astype(bf16)
    shared = jnp.concatenate([value_up_part, arrived[rows:]], axis=0)
    blocks = down_blocks(blocks_kernel, (rank_v,), (tokens,), devices, q_blocks, shared)
    blocks = lax.all_to_all(blocks, "ctx", 0, 0, tiled=True)
    summed = jnp.sum(blocks[:, : 3 * rank].astype(f32), axis=0)
    grad_down = jnp.sum(spread(summed[: 2 * rank].astype(bf16), "fsdp").astype(f32), axis=0)
    value_up_gradient = summed[2 * rank :]
    query_up = blocks[:, 3 * rank :].astype(f32)
    query_up = query_up.reshape(planes, chips, 2, rank // chips, half).sum(axis=0)
    query_up_gradient = query_up.transpose(0, 2, 1, 3).reshape(rank, width)
    return (attention, value_gradient, grad_down.T, query_up_gradient, value_up_gradient)


def solution(mesh):
    in_specs = (
        P("ctx", None),
        P("ctx", "fsdp"),
        P("ctx", "fsdp"),
        P("ctx", "fsdp"),
        P("ctx", None),
        P(None, "fsdp"),
        P(None, "fsdp"),
        P("fsdp"),
        P("ctx", "fsdp"),
    )
    out_specs = (
        P("ctx", "fsdp"),
        P("ctx", "fsdp"),
        P("ctx", None),
        P(None, "fsdp"),
        P(None, "fsdp"),
    )
    return jax.shard_map(
        on_device, mesh=mesh, in_specs=in_specs, out_specs=out_specs, check_vma=False
    )
```

```python
import functools

import jax
import jax.numpy as jnp
from jax import lax
from jax.experimental import pallas as pl
from jax.experimental.pallas import tpu as pltpu
from jax.sharding import PartitionSpec as P

GROUP = 2048
bf16 = jnp.bfloat16
f32 = jnp.float32
NT = (((1,), (1,)), ((), ()))
TN = (((0,), (0,)), ((), ()))


def spread(value, axis, groups=None):
    count = len(groups[0]) if groups else lax.axis_size(axis)
    copies = jnp.broadcast_to(value[None], (count, *value.shape))
    return lax.all_to_all(copies, axis, 0, 0, tiled=True, axis_index_groups=groups)


def to_chip(value, chips, other_core):
    count = lax.axis_size("ctx")
    pairs = []
    for source in range(count):
        core = source % 2
        target = (source - core + 2 * chips) % count + (1 - core if other_core else core)
        pairs.append((source, target))
    return lax.ppermute(value, "ctx", pairs)


def attention_kernel(
    scale, tile, info, tokens, theirs, weight, start, grad_out, kv,
    out, grad_query, grad_value, query, rows_in, arrivals,
):
    rows, size = query.shape[0], kv.shape[-1]
    heads = query.shape[1] // size
    blocks, block = kv.shape[1:3]
    keys = [kv.at[info[heads], d] for d in range(blocks)]
    values = [kv.at[1 - info[heads], d] for d in range(blocks)]
    parts, depth = rows_in.shape[:2]
    copies = []
    for i in range(parts):
        here = pl.ds(i * depth, depth)
        copies.append(pltpu.make_async_copy(weight.at[here], rows_in.at[i], arrivals.at[i]))
    for copy in copies:
        copy.start()
    grad_value[...] = jnp.zeros_like(grad_value)
    core, each = info[heads], rows // 2
    mine = pl.ds(pl.multiple_of(core * each, each), each)
    other = pl.ds(pl.multiple_of((1 - core) * each, each), each)
    totals = [start[mine, :], start[other, :]]
    for i, copy in enumerate(copies):
        copy.wait()
        here = slice(i * depth, (i + 1) * depth)
        for which, source in enumerate((tokens, theirs)):
            totals[which] += jnp.dot(source[:, here], rows_in[i], preferred_element_type=f32)
    query[mine, :] = totals[0].astype(bf16)
    query[other, :] = totals[1].astype(bf16)

    def tile_of(index, columns, count):
        here = pl.ds(pl.multiple_of(index * tile, tile), tile)
        q = query[here, columns]
        do = grad_out[here, columns]
        row = index * tile + lax.broadcasted_iota(jnp.int32, (tile, block), 0)
        column = lax.broadcasted_iota(jnp.int32, (tile, block), 1)
        scores = [
            lax.dot_general(q, keys[d][...], NT, preferred_element_type=f32) * scale
            for d in range(count)
        ]
        scores[0] = jnp.where(column <= row, scores[0], -1e30)
        highest = functools.reduce(
            jnp.maximum, [jnp.max(s, axis=1, keepdims=True) for s in scores]
        )
        weights = [jnp.exp(s - highest) for s in scores]
        inverse = 1.0 / functools.reduce(
            jnp.add, [jnp.sum(w, axis=1, keepdims=True) for w in weights]
        )
        probs = [w * inverse for w in weights]
        low = [p.astype(bf16) for p in probs]
        result = functools.reduce(
            jnp.add,
            [
                jnp.dot(low[d], values[d][...], preferred_element_type=f32)
                for d in range(count)
            ],
        ).astype(bf16)
        out[here, columns] = result
        correction = jnp.sum(do.astype(f32) * result.astype(f32), axis=1, keepdims=True)
        total = jnp.zeros((tile, size), f32)
        for d in range(count):
            grad_value[d] += lax.dot_general(low[d], do, TN, preferred_element_type=f32)
            grad_probs = lax.dot_general(do, values[d][...], NT, preferred_element_type=f32)
            grad_scores = (probs[d] * (grad_probs - correction)).astype(bf16)
            total = total + jnp.dot(grad_scores, keys[d][...], preferred_element_type=f32)
        grad_query[here, columns] = (total * scale).astype(bf16)

    for head in range(heads):
        columns = slice(head * size, (head + 1) * size)
        for count in range(1, blocks + 1):

            @pl.when(info[head] + 1 == count)
            def _(columns=columns, count=count):
                def step(index, carry):
                    tile_of(index, columns, count)
                    return carry

                lax.fori_loop(0, rows // tile, step, 0)


def attend(info, tokens, theirs, weight, start, grad_out, kv, tile=256, parts=8):
    rows, width = start.shape
    model = tokens.shape[1]
    size = kv.shape[-1]
    blocks, block = kv.shape[1:3]
    vmem = pl.BlockSpec(memory_space=pltpu.VMEM)
    return pl.pallas_call(
        functools.partial(attention_kernel, size ** (-0.5), tile),
        out_shape=(
            jax.ShapeDtypeStruct((rows, width), bf16),
            jax.ShapeDtypeStruct((rows, width), bf16),
            jax.ShapeDtypeStruct((blocks, block, size), f32),
        ),
        in_specs=[
            pl.BlockSpec(memory_space=pltpu.SMEM),
            vmem,
            vmem,
            pl.BlockSpec(memory_space=pl.ANY),
            vmem,
            vmem,
            vmem,
        ],
        out_specs=(vmem, vmem, vmem),
        scratch_shapes=[
            pltpu.VMEM((rows, width), bf16),
            pltpu.VMEM((parts, model // parts, width), bf16),
            pltpu.SemaphoreType.DMA((parts,)),
        ],
        compiler_params=pltpu.CompilerParams(vmem_limit_bytes=30 * 1024 * 1024),
        cost_estimate=pl.CostEstimate(
            flops=10 * rows * width * blocks * block + 2 * rows * width * model,
            bytes_accessed=16 * 1024 * 1024,
            transcendentals=rows * width // size * blocks * block,
        ),
        name="attention",
    )(info, tokens, theirs, weight, start, grad_out, kv)


def column_copies(sources, buffer, arrivals):
    parts, width = buffer.shape[0], buffer.shape[-1]
    copies = [
        [
            pltpu.make_async_copy(
                source.at[:, pl.ds(i * width, width)],
                buffer.at[i, which],
                arrivals.at[len(sources) * i + which],
            )
            for which, source in enumerate(sources)
        ]
        for i in range(parts)
    ]
    for copy in sum(copies, []):
        copy.start()
    return copies


def multiply_parts(ranks, copies, buffer, store):
    for i, part in enumerate(copies):
        for copy in part:
            copy.wait()
        product = functools.reduce(
            jnp.add,
            [
                jnp.dot(r, buffer[i, which], preferred_element_type=f32)
                for which, r in enumerate(ranks)
            ],
        ).astype(bf16)
        store(i, product)


def query_blocks_kernel(rank_mine, rank_theirs, tokens, theirs, out, buffer, arrivals):
    copies = column_copies((tokens, theirs), buffer, arrivals)
    size = out.shape[2]
    each = buffer.shape[-1] // size

    def store(i, product):
        for j in range(each):
            out[i * each + j] = product[:, j * size : (j + 1) * size]

    multiply_parts((rank_mine[...], rank_theirs[...]), copies, buffer, store)


def query_blocks(rank_mine, rank_theirs, tokens, theirs, devices, parts=4):
    rows, model = tokens.shape
    vmem = pl.BlockSpec(memory_space=pltpu.VMEM)
    anywhere = pl.BlockSpec(memory_space=pl.ANY)
    ranks = rank_mine.shape[0]
    return pl.pallas_call(
        query_blocks_kernel,
        out_shape=jax.ShapeDtypeStruct((devices, ranks, model // devices), bf16),
        in_specs=[vmem, vmem, anywhere, anywhere],
        out_specs=vmem,
        scratch_shapes=[
            pltpu.VMEM((parts, 2, rows, model // parts), bf16),
            pltpu.SemaphoreType.DMA((2 * parts,)),
        ],
        compiler_params=pltpu.CompilerParams(vmem_limit_bytes=40 * 1024 * 1024),
        cost_estimate=pl.CostEstimate(
            flops=4 * ranks * rows * model, bytes_accessed=4 * rows * model, transcendentals=0
        ),
        name="query_blocks",
    )(rank_mine, rank_theirs, tokens, theirs)


def all_blocks_kernel(own, *refs):
    arrived, (up, low, above, tokens, out, gradient, buffer, arrivals) = refs[:-8], refs[-8:]
    copies = column_copies((tokens,), buffer, arrivals)
    rows, size = gradient.shape
    each = buffer.shape[-1] // size
    total = own[...]
    for other in arrived:
        total += other[...].astype(f32)
    total = total.astype(bf16)
    mine = total[:rows]
    gradient[...] = mine
    ranks = lax.dot_general(up[...], mine, NT, preferred_element_type=f32).astype(bf16)
    up_part = lax.dot_general(low[...], mine, TN, preferred_element_type=f32).astype(bf16)
    top = above.shape[1]
    bottom = top + ranks.shape[0]
    last = bottom + up_part.shape[0]

    def store(i, product):
        for j in range(each):
            block = i * each + j
            out[block, :top] = above[block]
            out[block, top:bottom] = product[:, j * size : (j + 1) * size]
            out[block, bottom:last] = up_part
            out[block, last:] = total[rows:]

    multiply_parts((ranks,), copies, buffer, store)


def all_blocks(own, arrived, up, low, above, tokens, parts=4):
    rows, model = tokens.shape
    devices, ranks, size = above.shape
    vmem = pl.BlockSpec(memory_space=pltpu.VMEM)
    height = 3 * ranks + own.shape[0] - rows
    return pl.pallas_call(
        all_blocks_kernel,
        out_shape=(
            jax.ShapeDtypeStruct((devices, height, size), bf16),
            jax.ShapeDtypeStruct((rows, size), bf16),
        ),
        in_specs=[vmem] * (4 + len(arrived)) + [pl.BlockSpec(memory_space=pl.ANY)],
        out_specs=(vmem, vmem),
        scratch_shapes=[
            pltpu.VMEM((parts, 1, rows, model // parts), bf16),
            pltpu.SemaphoreType.DMA((parts,)),
        ],
        compiler_params=pltpu.CompilerParams(vmem_limit_bytes=40 * 1024 * 1024),
        cost_estimate=pl.CostEstimate(
            flops=2 * ranks * rows * model, bytes_accessed=3 * rows * model, transcendentals=0
        ),
        name="all_blocks",
    )(own, *arrived, up, low, above, tokens)


def on_device(
    tokens,
    query_weight,
    key_weight,
    value_weight,
    adapter_down_weight,
    query_up_weight,
    value_up_weight,
    head_shifts,
    output_gradient,
):
    rows, model = tokens.shape
    heads = head_shifts.shape[0]
    width = query_weight.shape[1]
    size = width // heads
    half = width // 2
    depth = query_weight.shape[0]
    rank = adapter_down_weight.shape[1] // 2
    devices = lax.axis_size("ctx")
    chips = GROUP // (2 * rows)
    members = 2 * chips
    position = lax.axis_index("ctx")
    core = lax.rem(position, 2)
    chip = lax.rem(lax.div(position, 2), chips)
    plain = [[start + i for i in range(members)] for start in range(0, devices, members)]
    across = [[g[i] for g in plain] for i in range(members)]
    planes = devices // members

    def both(mine, theirs):
        return jnp.concatenate(
            [jnp.where(core == 0, mine, theirs), jnp.where(core == 0, theirs, mine)], axis=0
        )

    def half_of(array, which):
        return lax.dynamic_slice_in_dim(array, which * (array.shape[0] // 2), array.shape[0] // 2)

    theirs = to_chip(tokens, 0, True)
    grad_halves = output_gradient.reshape(rows, 2, half).transpose(1, 0, 2)
    grad_mine = lax.dynamic_index_in_dim(grad_halves, core, 0, keepdims=False)
    grad_away = lax.dynamic_index_in_dim(grad_halves, 1 - core, 0, keepdims=False)
    grad_out = both(grad_mine, to_chip(grad_away, 0, True))

    down = adapter_down_weight.T
    kv_rows = jnp.stack(
        [
            jnp.concatenate([key_weight.T, down[:rank]]),
            jnp.concatenate([value_weight.T, down[rank:]]),
        ]
    )
    kv_rows = jnp.broadcast_to(kv_rows[None], (chips, *kv_rows.shape))
    kv_rows = lax.all_to_all(
        kv_rows.reshape(members, size + rank, depth),
        "ctx", 0, 0, tiled=True, axis_index_groups=plain,
    )
    kv_rows = lax.all_gather(kv_rows, "ctx", axis=0, tiled=True, axis_index_groups=across)
    q_rows = jnp.stack([query_weight[:, :half], query_weight[:, half:]])
    q_rows = jnp.broadcast_to(q_rows[None], (chips, *q_rows.shape))
    q_rows = lax.all_to_all(
        q_rows.reshape(members, depth, half),
        "ctx", 0, 0, tiled=True, axis_index_groups=plain,
    )
    q_rows = lax.all_gather(
        q_rows.reshape(members * depth, half),
        "ctx", axis=0, tiled=True, axis_index_groups=across,
    )

    kv_weight = kv_rows.transpose(1, 0, 2).reshape(size + rank, model)
    mine = both(
        lax.dot_general(tokens, kv_weight, NT, preferred_element_type=f32),
        lax.dot_general(theirs, kv_weight, NT, preferred_element_type=f32),
    )
    low = mine[:, size:].astype(bf16)
    extra = jnp.dot(low, value_up_weight, preferred_element_type=f32)
    mine = (mine[:, :size] + jnp.where(core == 1, extra, 0.0)).astype(bf16)
    low_away = to_chip(low, 0, True)
    low_q = jnp.where(core == 0, low, low_away)
    low_v = jnp.where(core == 0, low_away, low)
    mine = jnp.stack([mine] + [to_chip(mine, d, False) for d in range(1, chips)])
    kv = jnp.stack([mine, to_chip(mine, 0, True)])

    up_mine = lax.dynamic_slice_in_dim(query_up_weight, core * half, half, axis=1)
    start = jnp.dot(low_q, up_mine, preferred_element_type=f32)
    shifts = lax.dynamic_slice_in_dim(head_shifts, core * (heads // 2), heads // 2)
    seen = jnp.where(shifts != 0, lax.rem(chip + chips // 2, chips), chip)
    info = jnp.concatenate([seen, core[None]]).astype(jnp.int32)
    output, grad_query, value_parts = attend(
        info, tokens, theirs, q_rows, start, grad_out, kv
    )

    attention_mine = half_of(output, core)
    attention_other = to_chip(half_of(output, 1 - core), 0, True)
    attention = jnp.concatenate(
        [
            jnp.where(core == 0, attention_mine, attention_other),
            jnp.where(core == 0, attention_other, attention_mine),
        ],
        axis=1,
    )

    query_up_part = lax.dot_general(low_q, grad_query, TN, preferred_element_type=f32)
    query_up_part = query_up_part.reshape(chips, -1, size)
    value_parts = value_parts.reshape(chips, 2, rows, size).astype(bf16)
    same = lax.dynamic_index_in_dim(value_parts, core, 1, keepdims=False)
    cross = lax.dynamic_index_in_dim(value_parts, 1 - core, 1, keepdims=False)
    value_parts = same.astype(f32) + to_chip(cross, 0, True).astype(f32)

    def with_share(d):
        share = lax.dynamic_index_in_dim(
            query_up_part, lax.rem(chip + chips - d, chips), 0, keepdims=False
        )
        return jnp.concatenate([value_parts[d], share], axis=0)

    arrived = [with_share(0)]
    arrived += [to_chip(with_share(d).astype(bf16), -d, False) for d in range(1, chips)]

    rank_q = lax.dot_general(up_mine, grad_query, NT, preferred_element_type=f32).astype(bf16)
    rank_q = rank_q + (value_parts[0, 0, 0] * 0).astype(bf16)
    rank_halves = rank_q.reshape(rank, 2, rows)
    rank_mine = lax.dynamic_index_in_dim(rank_halves, core, 1, keepdims=False)
    rank_theirs = lax.dynamic_index_in_dim(rank_halves, 1 - core, 1, keepdims=False)
    blocks = query_blocks(rank_mine, rank_theirs, tokens, theirs, devices)
    blocks, value_gradient = all_blocks(
        arrived[0], arrived[1:], value_up_weight, half_of(low_v, core), blocks, tokens
    )
    blocks = lax.all_to_all(blocks, "ctx", 0, 0, tiled=True)
    summed = jnp.sum(blocks[:, : 3 * rank].astype(f32), axis=0)
    grad_down = jnp.sum(spread(summed[: 2 * rank].astype(bf16), "fsdp").astype(f32), axis=0)
    value_up_gradient = summed[2 * rank :]
    query_up = blocks[:, 3 * rank :].astype(f32)
    query_up = query_up.reshape(planes, chips, 2, rank // chips, half).sum(axis=0)
    query_up_gradient = query_up.transpose(0, 2, 1, 3).reshape(rank, width)
    return (attention, value_gradient, grad_down.T, query_up_gradient, value_up_gradient)


def solution(mesh):
    in_specs = (
        P("ctx", None),
        P("ctx", "fsdp"),
        P("ctx", "fsdp"),
        P("ctx", "fsdp"),
        P("ctx", None),
        P(None, "fsdp"),
        P(None, "fsdp"),
        P("fsdp"),
        P("ctx", "fsdp"),
    )
    out_specs = (
        P("ctx", "fsdp"),
        P("ctx", "fsdp"),
        P("ctx", None),
        P(None, "fsdp"),
        P(None, "fsdp"),
    )
    return jax.shard_map(
        on_device, mesh=mesh, in_specs=in_specs, out_specs=out_specs, check_vma=False
    )
```

```python
import functools

import jax
import jax.numpy as jnp
from jax import lax
from jax.experimental import pallas as pl
from jax.experimental.pallas import tpu as pltpu
from jax.sharding import PartitionSpec as P

GROUP = 2048
bf16 = jnp.bfloat16
f32 = jnp.float32
NT = (((1,), (1,)), ((), ()))
TN = (((0,), (0,)), ((), ()))


def spread(value, axis, groups=None):
    count = len(groups[0]) if groups else lax.axis_size(axis)
    copies = jnp.broadcast_to(value[None], (count, *value.shape))
    return lax.all_to_all(copies, axis, 0, 0, tiled=True, axis_index_groups=groups)


def to_chip(value, chips, other_core):
    count = lax.axis_size("ctx")
    pairs = []
    for source in range(count):
        core = source % 2
        target = (source - core + 2 * chips) % count + (1 - core if other_core else core)
        pairs.append((source, target))
    return lax.ppermute(value, "ctx", pairs)


def rows_of(tokens, theirs, columns, core, target, arrivals, first):
    rows = tokens.shape[0]
    mine = target.at[pl.ds(pl.multiple_of(core * rows, rows), rows)]
    other = target.at[pl.ds(pl.multiple_of((1 - core) * rows, rows), rows)]
    return [
        pltpu.make_async_copy(tokens.at[:, columns], mine, arrivals.at[first]),
        pltpu.make_async_copy(theirs.at[:, columns], other, arrivals.at[first + 1]),
    ]


def attention_kernel(
    scale, tile, info, tokens, theirs, weight, start, grad_out, kv,
    out, grad_query, grad_value, query, columns_in, rows_in, arrivals,
):
    rows, size = query.shape[0], kv.shape[-1]
    heads = query.shape[1] // size
    blocks, block = kv.shape[1:3]
    keys = [kv.at[info[heads], d] for d in range(blocks)]
    values = [kv.at[1 - info[heads], d] for d in range(blocks)]
    parts, depth = rows_in.shape[:2]
    copies = []
    for i in range(parts):
        here = pl.ds(i * depth, depth)
        copies.append(
            rows_of(tokens, theirs, here, info[heads], columns_in.at[i], arrivals, 3 * i)
            + [pltpu.make_async_copy(weight.at[here], rows_in.at[i], arrivals.at[3 * i + 2])]
        )
    for copy in sum(copies, []):
        copy.start()
    grad_value[...] = jnp.zeros_like(grad_value)
    total = start[...]
    for i in range(parts):
        for copy in copies[i]:
            copy.wait()
        total = total + jnp.dot(columns_in[i], rows_in[i], preferred_element_type=f32)
    query[...] = total.astype(bf16)

    def tile_of(index, columns, count):
        here = pl.ds(pl.multiple_of(index * tile, tile), tile)
        q = query[here, columns]
        do = grad_out[here, columns]
        row = index * tile + lax.broadcasted_iota(jnp.int32, (tile, block), 0)
        column = lax.broadcasted_iota(jnp.int32, (tile, block), 1)
        scores = [
            lax.dot_general(q, keys[d][...], NT, preferred_element_type=f32) * scale
            for d in range(count)
        ]
        scores[0] = jnp.where(column <= row, scores[0], -1e30)
        highest = functools.reduce(
            jnp.maximum, [jnp.max(s, axis=1, keepdims=True) for s in scores]
        )
        weights = [jnp.exp(s - highest) for s in scores]
        inverse = 1.0 / functools.reduce(
            jnp.add, [jnp.sum(w, axis=1, keepdims=True) for w in weights]
        )
        probs = [w * inverse for w in weights]
        low = [p.astype(bf16) for p in probs]
        result = functools.reduce(
            jnp.add,
            [
                jnp.dot(low[d], values[d][...], preferred_element_type=f32)
                for d in range(count)
            ],
        ).astype(bf16)
        out[here, columns] = result
        correction = jnp.sum(do.astype(f32) * result.astype(f32), axis=1, keepdims=True)
        total = jnp.zeros((tile, size), f32)
        for d in range(count):
            grad_value[d] += lax.dot_general(low[d], do, TN, preferred_element_type=f32)
            grad_probs = lax.dot_general(do, values[d][...], NT, preferred_element_type=f32)
            grad_scores = (probs[d] * (grad_probs - correction)).astype(bf16)
            total = total + jnp.dot(grad_scores, keys[d][...], preferred_element_type=f32)
        grad_query[here, columns] = (total * scale).astype(bf16)

    for head in range(heads):
        columns = slice(head * size, (head + 1) * size)
        for count in range(1, blocks + 1):

            @pl.when(info[head] + 1 == count)
            def _(columns=columns, count=count):
                def step(index, carry):
                    tile_of(index, columns, count)
                    return carry

                lax.fori_loop(0, rows // tile, step, 0)


def attend(info, tokens, theirs, weight, start, grad_out, kv, tile=256, parts=8):
    rows, width = start.shape
    model = tokens.shape[1]
    size = kv.shape[-1]
    blocks, block = kv.shape[1:3]
    vmem = pl.BlockSpec(memory_space=pltpu.VMEM)
    return pl.pallas_call(
        functools.partial(attention_kernel, size ** (-0.5), tile),
        out_shape=(
            jax.ShapeDtypeStruct((rows, width), bf16),
            jax.ShapeDtypeStruct((rows, width), bf16),
            jax.ShapeDtypeStruct((blocks, block, size), f32),
        ),
        in_specs=[
            pl.BlockSpec(memory_space=pltpu.SMEM),
            pl.BlockSpec(memory_space=pl.ANY),
            pl.BlockSpec(memory_space=pl.ANY),
            pl.BlockSpec(memory_space=pl.ANY),
            vmem,
            vmem,
            vmem,
        ],
        out_specs=(vmem, vmem, vmem),
        scratch_shapes=[
            pltpu.VMEM((rows, width), bf16),
            pltpu.VMEM((parts, rows, model // parts), bf16),
            pltpu.VMEM((parts, model // parts, width), bf16),
            pltpu.SemaphoreType.DMA((3 * parts,)),
        ],
        compiler_params=pltpu.CompilerParams(vmem_limit_bytes=48 * 1024 * 1024),
        cost_estimate=pl.CostEstimate(
            flops=10 * rows * width * blocks * block + 2 * rows * width * model,
            bytes_accessed=16 * 1024 * 1024,
            transcendentals=rows * width // size * blocks * block,
        ),
        name="attention",
    )(info, tokens, theirs, weight, start, grad_out, kv)


def all_blocks_kernel(info, own, *refs):
    arrived, refs = refs[:-9], refs[-9:]
    up, low, rank_q, tokens, theirs, out, gradient, buffer, arrivals = refs
    core = info[0]
    size = gradient.shape[1]
    each = buffer.shape[-1] // size
    copies = []
    for block in range(out.shape[0]):
        part, lane = block // each, block % each * size
        columns = pl.ds(pl.multiple_of((2 * block + core) * size, size), size)
        target = buffer.at[part, :, pl.ds(lane, size)]
        copies.append(rows_of(tokens, theirs, columns, core, target, arrivals, 2 * block))
    for copy in sum(copies, []):
        copy.start()
    rows = gradient.shape[0]
    total = own[...]
    for other in arrived:
        total += other[...].astype(f32)
    total = total.astype(bf16)
    mine = total[:rows]
    gradient[...] = mine
    rank_v = lax.dot_general(up[...], mine, NT, preferred_element_type=f32).astype(bf16)
    ranks = jnp.concatenate([rank_q[...], rank_v], axis=0)
    up_part = lax.dot_general(low[...], mine, TN, preferred_element_type=f32).astype(bf16)
    bottom = ranks.shape[0]
    last = bottom + up_part.shape[0]
    for part in range(buffer.shape[0]):
        for copy in sum(copies[part * each : (part + 1) * each], []):
            copy.wait()
        product = jnp.dot(ranks, buffer[part], preferred_element_type=f32).astype(bf16)
        for j in range(each):
            block = part * each + j
            out[block, :bottom] = product[:, j * size : (j + 1) * size]
            out[block, bottom:last] = up_part
            out[block, last:] = total[rows:]


def all_blocks(info, own, arrived, up, low, rank_q, tokens, theirs, parts=4):
    rows, model = tokens.shape
    ranks, size = up.shape
    count = model // (2 * size)
    vmem = pl.BlockSpec(memory_space=pltpu.VMEM)
    anywhere = pl.BlockSpec(memory_space=pl.ANY)
    height = 3 * ranks + own.shape[0] - 2 * rows
    return pl.pallas_call(
        all_blocks_kernel,
        out_shape=(
            jax.ShapeDtypeStruct((count, height, size), bf16),
            jax.ShapeDtypeStruct((2 * rows, size), bf16),
        ),
        in_specs=[pl.BlockSpec(memory_space=pltpu.SMEM)]
        + [vmem] * (4 + len(arrived))
        + [anywhere, anywhere],
        out_specs=(vmem, vmem),
        scratch_shapes=[
            pltpu.VMEM((parts, 2 * rows, model // (2 * parts)), bf16),
            pltpu.SemaphoreType.DMA((2 * count,)),
        ],
        compiler_params=pltpu.CompilerParams(vmem_limit_bytes=56 * 1024 * 1024),
        cost_estimate=pl.CostEstimate(
            flops=4 * ranks * rows * model, bytes_accessed=3 * rows * model, transcendentals=0
        ),
        name="all_blocks",
    )(info, own, *arrived, up, low, rank_q, tokens, theirs)


def on_device(
    tokens,
    query_weight,
    key_weight,
    value_weight,
    adapter_down_weight,
    query_up_weight,
    value_up_weight,
    head_shifts,
    output_gradient,
):
    rows, model = tokens.shape
    heads = head_shifts.shape[0]
    width = query_weight.shape[1]
    size = width // heads
    half = width // 2
    depth = query_weight.shape[0]
    rank = adapter_down_weight.shape[1] // 2
    devices = lax.axis_size("ctx")
    chips = GROUP // (2 * rows)
    members = 2 * chips
    position = lax.axis_index("ctx")
    core = lax.rem(position, 2)
    chip = lax.rem(lax.div(position, 2), chips)
    plain = [[start + i for i in range(members)] for start in range(0, devices, members)]
    across = [[g[i] for g in plain] for i in range(members)]
    planes = devices // members

    def both(mine, theirs):
        return jnp.concatenate(
            [jnp.where(core == 0, mine, theirs), jnp.where(core == 0, theirs, mine)], axis=0
        )

    def half_of(array, which):
        return lax.dynamic_slice_in_dim(array, which * (array.shape[0] // 2), array.shape[0] // 2)

    theirs = to_chip(tokens, 0, True)
    grad_halves = output_gradient.reshape(rows, 2, half).transpose(1, 0, 2)
    grad_mine = lax.dynamic_index_in_dim(grad_halves, core, 0, keepdims=False)
    grad_away = lax.dynamic_index_in_dim(grad_halves, 1 - core, 0, keepdims=False)
    grad_out = both(grad_mine, to_chip(grad_away, 0, True))

    down = adapter_down_weight.T
    kv_rows = jnp.stack(
        [
            jnp.concatenate([key_weight.T, down[:rank]]),
            jnp.concatenate([value_weight.T, down[rank:]]),
        ]
    )
    kv_rows = jnp.broadcast_to(kv_rows[None], (chips, *kv_rows.shape))
    kv_rows = lax.all_to_all(
        kv_rows.reshape(members, size + rank, depth),
        "ctx", 0, 0, tiled=True, axis_index_groups=plain,
    )
    kv_rows = lax.all_gather(kv_rows, "ctx", axis=0, tiled=True, axis_index_groups=across)
    q_rows = jnp.stack([query_weight[:, :half], query_weight[:, half:]])
    q_rows = jnp.broadcast_to(q_rows[None], (chips, *q_rows.shape))
    q_rows = lax.all_to_all(
        q_rows.reshape(members, depth, half),
        "ctx", 0, 0, tiled=True, axis_index_groups=plain,
    )
    q_rows = lax.all_gather(
        q_rows.reshape(members * depth, half),
        "ctx", axis=0, tiled=True, axis_index_groups=across,
    )

    kv_weight = kv_rows.transpose(1, 0, 2).reshape(size + rank, model)
    mine = both(
        lax.dot_general(tokens, kv_weight, NT, preferred_element_type=f32),
        lax.dot_general(theirs, kv_weight, NT, preferred_element_type=f32),
    )
    low = mine[:, size:].astype(bf16)
    extra = jnp.dot(low, value_up_weight, preferred_element_type=f32)
    mine = (mine[:, :size] + jnp.where(core == 1, extra, 0.0)).astype(bf16)
    low_away = to_chip(low, 0, True)
    low_q = jnp.where(core == 0, low, low_away)
    low_v = jnp.where(core == 0, low_away, low)
    mine = jnp.stack([mine] + [to_chip(mine, d, False) for d in range(1, chips)])
    kv = jnp.stack([mine, to_chip(mine, 0, True)])

    up_mine = lax.dynamic_slice_in_dim(query_up_weight, core * half, half, axis=1)
    start = jnp.dot(low_q, up_mine, preferred_element_type=f32)
    shifts = lax.dynamic_slice_in_dim(head_shifts, core * (heads // 2), heads // 2)
    seen = jnp.where(shifts != 0, lax.rem(chip + chips // 2, chips), chip)
    info = jnp.concatenate([seen, core[None]]).astype(jnp.int32)
    output, grad_query, value_parts = attend(
        info, tokens, theirs, q_rows, start, grad_out, kv
    )

    attention_mine = half_of(output, core)
    attention_other = to_chip(half_of(output, 1 - core), 0, True)
    attention = jnp.concatenate(
        [
            jnp.where(core == 0, attention_mine, attention_other),
            jnp.where(core == 0, attention_other, attention_mine),
        ],
        axis=1,
    )

    count = value_parts.shape[0] * value_parts.shape[1]
    query_up_part = lax.dot_general(low_q, grad_query, TN, preferred_element_type=f32)
    rank_q = lax.dot_general(up_mine, grad_query, NT, preferred_element_type=f32)
    swapped = [value_parts, query_up_part, rank_q]
    swapped = jnp.concatenate([part.astype(bf16).reshape(-1, size) for part in swapped])
    swapped = [swapped, to_chip(swapped, 0, True)]
    value_parts = (swapped[0][:count].astype(f32) + swapped[1][:count].astype(f32)).reshape(
        value_parts.shape
    )
    last = count + rank * half // size
    rank_q = [part[last:].reshape(rank, -1).astype(f32) for part in swapped]
    rank_q = (rank_q[0] + rank_q[1]).astype(bf16)
    query_up_part = [part[count:last].reshape(rank, half) for part in swapped]
    query_up_part = jnp.concatenate(
        [jnp.where(core == 0, *query_up_part), jnp.where(core == 0, *query_up_part[::-1])], axis=1
    ).reshape(chips, -1, size)

    def with_share(d):
        share = lax.dynamic_index_in_dim(
            query_up_part, lax.rem(chip + chips - d, chips), 0, keepdims=False
        )
        return jnp.concatenate([value_parts[d].astype(bf16), share], axis=0)

    arrived = [to_chip(with_share(d), -d, False) for d in range(1, chips)]

    blocks, value_gradient = all_blocks(
        core[None].astype(jnp.int32),
        with_share(0).astype(f32),
        arrived,
        value_up_weight,
        low_v,
        rank_q,
        tokens,
        theirs,
    )
    same_core = [[i for i in range(devices) if i % 2 == c] for c in range(2)]
    blocks = lax.all_to_all(
        blocks, "ctx", 0, 0, tiled=True, axis_index_groups=same_core
    )
    summed = jnp.sum(blocks[:, : 3 * rank].astype(f32), axis=0)
    grad_down = jnp.sum(spread(summed[: 2 * rank].astype(bf16), "fsdp").astype(f32), axis=0)
    value_up_gradient = summed[2 * rank :]
    query_up = blocks[:, 3 * rank :].astype(f32)
    query_up = query_up.reshape(planes, chips, -1, size).sum(axis=0)
    query_up_gradient = query_up.reshape(rank, width)
    return (
        attention,
        half_of(value_gradient, core),
        grad_down.T,
        query_up_gradient,
        value_up_gradient,
    )


def solution(mesh):
    in_specs = (
        P("ctx", None),
        P("ctx", "fsdp"),
        P("ctx", "fsdp"),
        P("ctx", "fsdp"),
        P("ctx", None),
        P(None, "fsdp"),
        P(None, "fsdp"),
        P("fsdp"),
        P("ctx", "fsdp"),
    )
    out_specs = (
        P("ctx", "fsdp"),
        P("ctx", "fsdp"),
        P("ctx", None),
        P(None, "fsdp"),
        P(None, "fsdp"),
    )
    return jax.shard_map(
        on_device, mesh=mesh, in_specs=in_specs, out_specs=out_specs, check_vma=False
    )
```

```python
import functools

import jax
import jax.numpy as jnp
from jax import lax
from jax.experimental import pallas as pl
from jax.experimental.pallas import tpu as pltpu
from jax.sharding import PartitionSpec as P

GROUP = 2048
bf16 = jnp.bfloat16
f32 = jnp.float32
NT = (((1,), (1,)), ((), ()))
TN = (((0,), (0,)), ((), ()))


def spread(value, axis, groups=None):
    count = len(groups[0]) if groups else lax.axis_size(axis)
    copies = jnp.broadcast_to(value[None], (count, *value.shape))
    return lax.all_to_all(copies, axis, 0, 0, tiled=True, axis_index_groups=groups)


def to_chip(value, chips, other_core):
    count = lax.axis_size("ctx")
    pairs = []
    for source in range(count):
        core = source % 2
        target = (source - core + 2 * chips) % count + (1 - core if other_core else core)
        pairs.append((source, target))
    return lax.ppermute(value, "ctx", pairs)


def rows_of(tokens, theirs, columns, core, target, arrivals, first):
    rows = tokens.shape[0]
    mine = target.at[pl.ds(pl.multiple_of(core * rows, rows), rows)]
    other = target.at[pl.ds(pl.multiple_of((1 - core) * rows, rows), rows)]
    return [
        pltpu.make_async_copy(tokens.at[:, columns], mine, arrivals.at[first]),
        pltpu.make_async_copy(theirs.at[:, columns], other, arrivals.at[first + 1]),
    ]


def attention_kernel(
    scale, tile, info, tokens, theirs, weight, start, grad_out, kv, ahead,
    out, grad_query, grad_value, query, columns_in, rows_in, arrivals,
):
    rows, size = query.shape[0], kv.shape[-1]
    heads = query.shape[1] // size
    blocks, block = kv.shape[1:3]
    keys = [kv.at[info[heads], d] for d in range(blocks)]
    values = [kv.at[1 - info[heads], d] for d in range(blocks)]
    parts, depth = rows_in.shape[:2]
    copies = []
    for i in range(parts):
        here = pl.ds(i * depth, depth)
        copies.append(
            rows_of(tokens, theirs, here, info[heads], columns_in.at[i], arrivals, 3 * i)
            + [pltpu.make_async_copy(weight.at[here], rows_in.at[i], arrivals.at[3 * i + 2])]
        )
    for copy in sum(copies, []):
        copy.start()
    grad_value[...] = jnp.zeros_like(grad_value)
    total = start[...]
    for i in range(parts):
        for copy in copies[i]:
            copy.wait()
        total = total + jnp.dot(columns_in[i], rows_in[i], preferred_element_type=f32)
    query[...] = total.astype(bf16)

    def tile_of(index, columns, count):
        here = slice(index * tile, (index + 1) * tile)
        widths = [here.stop] + [block] * (count - 1)
        q = query[here, columns]
        do = grad_out[here, columns]
        row = index * tile + lax.broadcasted_iota(jnp.int32, (tile, here.stop), 0)
        column = lax.broadcasted_iota(jnp.int32, (tile, here.stop), 1)
        scores = [
            lax.dot_general(q, keys[d][:w], NT, preferred_element_type=f32) * scale
            for d, w in enumerate(widths)
        ]
        scores[0] = jnp.where(column <= row, scores[0], -1e30)
        highest = functools.reduce(
            jnp.maximum, [jnp.max(s, axis=1, keepdims=True) for s in scores]
        )
        weights = [jnp.exp(s - highest) for s in scores]
        inverse = 1.0 / functools.reduce(
            jnp.add, [jnp.sum(w, axis=1, keepdims=True) for w in weights]
        )
        probs = [w * inverse for w in weights]
        low = [p.astype(bf16) for p in probs]
        result = functools.reduce(
            jnp.add,
            [
                jnp.dot(low[d], values[d][:w], preferred_element_type=f32)
                for d, w in enumerate(widths)
            ],
        ).astype(bf16)
        out[here, columns] = result
        correction = jnp.sum(do.astype(f32) * result.astype(f32), axis=1, keepdims=True)
        total = jnp.zeros((tile, size), f32)
        for d, w in enumerate(widths):
            grad_value[d, :w] += lax.dot_general(low[d], do, TN, preferred_element_type=f32)
            grad_probs = lax.dot_general(do, values[d][:w], NT, preferred_element_type=f32)
            grad_scores = (probs[d] * (grad_probs - correction)).astype(bf16)
            total = total + jnp.dot(grad_scores, keys[d][:w], preferred_element_type=f32)
        grad_query[here, columns] = (total * scale).astype(bf16)

    for head in range(heads):
        columns = slice(head * size, (head + 1) * size)
        for count in range(1, blocks + 1):

            @pl.when(info[head] + 1 == count)
            def _(columns=columns, count=count):
                for index in range(rows // tile):
                    tile_of(index, columns, count)


def attend(info, tokens, theirs, weight, start, grad_out, kv, ahead, tile=256, parts=8):
    rows, width = start.shape
    model = tokens.shape[1]
    size = kv.shape[-1]
    blocks, block = kv.shape[1:3]
    vmem = pl.BlockSpec(memory_space=pltpu.VMEM)
    return pl.pallas_call(
        functools.partial(attention_kernel, size ** (-0.5), tile),
        out_shape=(
            jax.ShapeDtypeStruct((rows, width), bf16),
            jax.ShapeDtypeStruct((rows, width), bf16),
            jax.ShapeDtypeStruct((blocks, block, size), f32),
        ),
        in_specs=[
            pl.BlockSpec(memory_space=pltpu.SMEM),
            pl.BlockSpec(memory_space=pl.ANY),
            pl.BlockSpec(memory_space=pl.ANY),
            pl.BlockSpec(memory_space=pl.ANY),
            vmem,
            vmem,
            vmem,
            pl.BlockSpec(memory_space=pl.ANY),
        ],
        out_specs=(vmem, vmem, vmem),
        scratch_shapes=[
            pltpu.VMEM((rows, width), bf16),
            pltpu.VMEM((parts, rows, model // parts), bf16),
            pltpu.VMEM((parts, model // parts, width), bf16),
            pltpu.SemaphoreType.DMA((3 * parts,)),
        ],
        compiler_params=pltpu.CompilerParams(vmem_limit_bytes=48 * 1024 * 1024),
        cost_estimate=pl.CostEstimate(
            flops=10 * rows * width * blocks * block + 2 * rows * width * model,
            bytes_accessed=16 * 1024 * 1024,
            transcendentals=rows * width // size * blocks * block,
        ),
        name="attention",
    )(info, tokens, theirs, weight, start, grad_out, kv, ahead)


def all_blocks_kernel(own, *refs):
    arrived, refs = refs[:-8], refs[-8:]
    up, low, rank_q, chip_columns, out, gradient, buffer, arrivals = refs
    size = gradient.shape[1]
    parts, rows, width = buffer.shape
    copies = [
        pltpu.make_async_copy(
            chip_columns.at[:, pl.ds(part * width, width)], buffer.at[part], arrivals.at[part]
        )
        for part in range(parts)
    ]
    for copy in copies:
        copy.start()
    total = own[...]
    for other in arrived:
        total += other[...].astype(f32)
    total = total.astype(bf16)
    mine = total[:rows]
    gradient[...] = mine
    rank_v = lax.dot_general(up[...], mine, NT, preferred_element_type=f32).astype(bf16)
    ranks = jnp.concatenate([rank_q[...], rank_v], axis=0)
    up_part = lax.dot_general(low[...], mine, TN, preferred_element_type=f32).astype(bf16)
    bottom = ranks.shape[0]
    last = bottom + up_part.shape[0]
    each = width // size
    for part in range(parts):
        copies[part].wait()
        product = jnp.dot(ranks, buffer[part], preferred_element_type=f32).astype(bf16)
        for j in range(each):
            block = part * each + j
            out[block, :bottom] = product[:, j * size : (j + 1) * size]
            out[block, bottom:last] = up_part
            out[block, last:] = total[rows:]


def all_blocks(own, arrived, up, low, rank_q, chip_columns, parts=4):
    rows, model = chip_columns.shape
    ranks, size = up.shape
    vmem = pl.BlockSpec(memory_space=pltpu.VMEM)
    height = 3 * ranks + own.shape[0] - rows
    return pl.pallas_call(
        all_blocks_kernel,
        out_shape=(
            jax.ShapeDtypeStruct((model // size, height, size), bf16),
            jax.ShapeDtypeStruct((rows, size), bf16),
        ),
        in_specs=[vmem] * (4 + len(arrived)) + [pl.BlockSpec(memory_space=pl.ANY)],
        out_specs=(vmem, vmem),
        scratch_shapes=[
            pltpu.VMEM((parts, rows, model // parts), bf16),
            pltpu.SemaphoreType.DMA((parts,)),
        ],
        compiler_params=pltpu.CompilerParams(vmem_limit_bytes=56 * 1024 * 1024),
        cost_estimate=pl.CostEstimate(
            flops=4 * ranks * rows * model, bytes_accessed=3 * rows * model, transcendentals=0
        ),
        name="all_blocks",
    )(own, *arrived, up, low, rank_q, chip_columns)


def on_device(
    tokens,
    query_weight,
    key_weight,
    value_weight,
    adapter_down_weight,
    query_up_weight,
    value_up_weight,
    head_shifts,
    output_gradient,
):
    rows, model = tokens.shape
    heads = head_shifts.shape[0]
    width = query_weight.shape[1]
    size = width // heads
    half = width // 2
    depth = query_weight.shape[0]
    rank = adapter_down_weight.shape[1] // 2
    devices = lax.axis_size("ctx")
    chips = GROUP // (2 * rows)
    members = 2 * chips
    position = lax.axis_index("ctx")
    core = lax.rem(position, 2)
    chip = lax.rem(lax.div(position, 2), chips)
    plain = [[start + i for i in range(members)] for start in range(0, devices, members)]
    across = [[g[i] for g in plain] for i in range(members)]
    planes = devices // members

    def both(mine, theirs):
        return jnp.concatenate(
            [jnp.where(core == 0, mine, theirs), jnp.where(core == 0, theirs, mine)], axis=0
        )

    def half_of(array, which):
        return lax.dynamic_slice_in_dim(array, which * (array.shape[0] // 2), array.shape[0] // 2)

    theirs = to_chip(tokens, 0, True)
    grad_halves = output_gradient.reshape(rows, 2, half).transpose(1, 0, 2)
    grad_mine = lax.dynamic_index_in_dim(grad_halves, core, 0, keepdims=False)
    grad_away = lax.dynamic_index_in_dim(grad_halves, 1 - core, 0, keepdims=False)
    grad_out = both(grad_mine, to_chip(grad_away, 0, True))

    down = adapter_down_weight.T
    kv_rows = jnp.stack(
        [
            jnp.concatenate([key_weight.T, down[:rank]]),
            jnp.concatenate([value_weight.T, down[rank:]]),
        ]
    )
    kv_rows = jnp.broadcast_to(kv_rows[None], (chips, *kv_rows.shape))
    kv_rows = lax.all_to_all(
        kv_rows.reshape(members, size + rank, depth),
        "ctx", 0, 0, tiled=True, axis_index_groups=plain,
    )
    kv_rows = lax.all_gather(kv_rows, "ctx", axis=0, tiled=True, axis_index_groups=across)
    q_rows = jnp.stack([query_weight[:, :half], query_weight[:, half:]])
    q_rows = jnp.broadcast_to(q_rows[None], (chips, *q_rows.shape))
    q_rows = lax.all_to_all(
        q_rows.reshape(members, depth, half),
        "ctx", 0, 0, tiled=True, axis_index_groups=plain,
    )
    q_rows = lax.all_gather(
        q_rows.reshape(members * depth, half),
        "ctx", axis=0, tiled=True, axis_index_groups=across,
    )

    kv_weight = kv_rows.transpose(1, 0, 2).reshape(size + rank, model)
    mine = both(
        lax.dot_general(tokens, kv_weight, NT, preferred_element_type=f32),
        lax.dot_general(theirs, kv_weight, NT, preferred_element_type=f32),
    )
    low = mine[:, size:].astype(bf16)
    extra = jnp.dot(low, value_up_weight, preferred_element_type=f32)
    mine = (mine[:, :size] + jnp.where(core == 1, extra, 0.0)).astype(bf16)
    low_away = to_chip(low, 0, True)
    low_q = jnp.where(core == 0, low, low_away)
    low_v = jnp.where(core == 0, low_away, low)
    mine = jnp.stack([mine] + [to_chip(mine, d, False) for d in range(1, chips)])
    kv = jnp.stack([mine, to_chip(mine, 0, True)])

    up_mine = lax.dynamic_slice_in_dim(query_up_weight, core * half, half, axis=1)
    start = jnp.dot(low_q, up_mine, preferred_element_type=f32)
    def own_columns(array):
        pairs = array.reshape(rows, devices // 2, 2, depth)
        return lax.dynamic_index_in_dim(pairs, core, 2, keepdims=False).reshape(rows, model // 2)

    chip_columns = both(own_columns(tokens), own_columns(theirs))
    shifts = lax.dynamic_slice_in_dim(head_shifts, core * (heads // 2), heads // 2)
    seen = jnp.where(shifts != 0, lax.rem(chip + chips // 2, chips), chip)
    info = jnp.concatenate([seen, core[None]]).astype(jnp.int32)
    output, grad_query, value_parts = attend(
        info, tokens, theirs, q_rows, start, grad_out, kv, chip_columns
    )

    attention_mine = half_of(output, core)
    attention_other = to_chip(half_of(output, 1 - core), 0, True)
    attention = jnp.concatenate(
        [
            jnp.where(core == 0, attention_mine, attention_other),
            jnp.where(core == 0, attention_other, attention_mine),
        ],
        axis=1,
    )

    count = value_parts.shape[0] * value_parts.shape[1]
    query_up_part = lax.dot_general(low_q, grad_query, TN, preferred_element_type=f32)
    rank_q = lax.dot_general(up_mine, grad_query, NT, preferred_element_type=f32)
    swapped = [value_parts, query_up_part, rank_q]
    swapped = jnp.concatenate([part.astype(bf16).reshape(-1, size) for part in swapped])
    swapped = [swapped, to_chip(swapped, 0, True)]
    value_parts = (swapped[0][:count].astype(f32) + swapped[1][:count].astype(f32)).reshape(
        value_parts.shape
    )
    last = count + rank * half // size
    rank_q = [part[last:].reshape(rank, -1).astype(f32) for part in swapped]
    rank_q = (rank_q[0] + rank_q[1]).astype(bf16)
    query_up_part = [part[count:last].reshape(rank, half) for part in swapped]
    query_up_part = jnp.concatenate(
        [jnp.where(core == 0, *query_up_part), jnp.where(core == 0, *query_up_part[::-1])], axis=1
    ).reshape(chips, -1, size)

    def with_share(d):
        share = lax.dynamic_index_in_dim(
            query_up_part, lax.rem(chip + chips - d, chips), 0, keepdims=False
        )
        return jnp.concatenate([value_parts[d].astype(bf16), share], axis=0)

    arrived = [to_chip(with_share(d), -d, False) for d in range(1, chips)]

    blocks, value_gradient = all_blocks(
        with_share(0).astype(f32),
        arrived,
        value_up_weight,
        low_v,
        rank_q,
        chip_columns,
    )
    same_core = [[i for i in range(devices) if i % 2 == c] for c in range(2)]
    blocks = lax.all_to_all(
        blocks, "ctx", 0, 0, tiled=True, axis_index_groups=same_core
    )
    summed = jnp.sum(blocks[:, : 3 * rank].astype(f32), axis=0)
    grad_down = jnp.sum(spread(summed[: 2 * rank].astype(bf16), "fsdp").astype(f32), axis=0)
    value_up_gradient = summed[2 * rank :]
    query_up = blocks[:, 3 * rank :].astype(f32)
    query_up = query_up.reshape(planes, chips, -1, size).sum(axis=0)
    query_up_gradient = query_up.reshape(rank, width)
    return (
        attention,
        half_of(value_gradient, core),
        grad_down.T,
        query_up_gradient,
        value_up_gradient,
    )


def solution(mesh):
    in_specs = (
        P("ctx", None),
        P("ctx", "fsdp"),
        P("ctx", "fsdp"),
        P("ctx", "fsdp"),
        P("ctx", None),
        P(None, "fsdp"),
        P(None, "fsdp"),
        P("fsdp"),
        P("ctx", "fsdp"),
    )
    out_specs = (
        P("ctx", "fsdp"),
        P("ctx", "fsdp"),
        P("ctx", None),
        P(None, "fsdp"),
        P(None, "fsdp"),
    )
    return jax.shard_map(
        on_device, mesh=mesh, in_specs=in_specs, out_specs=out_specs, check_vma=False
    )
```

```python
import functools

import jax
import jax.numpy as jnp
from jax import lax
from jax.experimental import pallas as pl
from jax.experimental.pallas import tpu as pltpu
from jax.sharding import PartitionSpec as P

GROUP = 2048
bf16 = jnp.bfloat16
f32 = jnp.float32
NT = (((1,), (1,)), ((), ()))
TN = (((0,), (0,)), ((), ()))


def to_chip(value, chips, other_core):
    count = lax.axis_size("ctx")
    pairs = []
    for source in range(count):
        core = source % 2
        target = (source - core + 2 * chips) % count + (1 - core if other_core else core)
        pairs.append((source, target))
    return lax.ppermute(value, "ctx", pairs)


def payload_kernel(key_weight, value_weight, down, out):
    size, rank = key_weight.shape[1], down.shape[0] // 2
    adapters = down[...]
    for core, weight in enumerate((key_weight, value_weight)):
        turned = weight[...].astype(f32).T.astype(bf16)
        for member in range(core, out.shape[0], 2):
            out[member, :size] = turned
            out[member, size:] = adapters[core * rank : (core + 1) * rank]


def payload(key_weight, value_weight, down, members):
    depth, size = key_weight.shape
    vmem = pl.BlockSpec(memory_space=pltpu.VMEM)
    return pl.pallas_call(
        payload_kernel,
        out_shape=jax.ShapeDtypeStruct((members, size + down.shape[0] // 2, depth), bf16),
        in_specs=[vmem] * 3,
        out_specs=vmem,
        name="payload",
    )(key_weight, value_weight, down)


def sum_kernel(blocks, copies, value_up, query_up):
    ranks, shares = copies.shape[1], query_up.shape[0]
    last = ranks + value_up.shape[0]
    total = blocks[0, :last].astype(f32)
    for chip in range(1, blocks.shape[0]):
        total += blocks[chip, :last].astype(f32)
    low = total[:ranks].astype(bf16)
    for copy in range(copies.shape[0]):
        copies[copy] = low
    value_up[...] = total[ranks:]
    for share in range(shares):
        total = blocks[share, last:].astype(f32)
        for chip in range(share + shares, blocks.shape[0], shares):
            total += blocks[chip, last:].astype(f32)
        query_up[share] = total


def sum_blocks(blocks, rank, count, shares):
    size = blocks.shape[2]
    vmem = pl.BlockSpec(memory_space=pltpu.VMEM)
    return pl.pallas_call(
        sum_kernel,
        out_shape=(
            jax.ShapeDtypeStruct((count, 2 * rank, size), bf16),
            jax.ShapeDtypeStruct((rank, size), f32),
            jax.ShapeDtypeStruct((shares, blocks.shape[1] - 3 * rank, size), f32),
        ),
        in_specs=[vmem],
        out_specs=(vmem, vmem, vmem),
        name="sum_blocks",
    )(blocks)


def rows_of(tokens, theirs, columns, core, target, arrivals, first):
    rows = tokens.shape[0]
    mine = target.at[pl.ds(pl.multiple_of(core * rows, rows), rows)]
    other = target.at[pl.ds(pl.multiple_of((1 - core) * rows, rows), rows)]
    return [
        pltpu.make_async_copy(tokens.at[:, columns], mine, arrivals.at[first]),
        pltpu.make_async_copy(theirs.at[:, columns], other, arrivals.at[first + 1]),
    ]


def attention_kernel(
    scale, tile, info, tokens, theirs, weight, start, grad_out, kv,
    out, grad_query, grad_value, query, columns_in, rows_in, arrivals,
):
    rows, size = query.shape[0], kv.shape[-1]
    heads = query.shape[1] // size
    blocks, block = kv.shape[1:3]
    keys = [kv.at[info[heads], d] for d in range(blocks)]
    values = [kv.at[1 - info[heads], d] for d in range(blocks)]
    parts, depth = rows_in.shape[:2]
    copies = []
    for i in range(parts):
        here = pl.ds(i * depth, depth)
        copies.append(
            rows_of(tokens, theirs, here, info[heads], columns_in.at[i], arrivals, 3 * i)
            + [pltpu.make_async_copy(weight.at[here], rows_in.at[i], arrivals.at[3 * i + 2])]
        )
    for copy in sum(copies, []):
        copy.start()
    grad_value[...] = jnp.zeros_like(grad_value)
    total = start[...]
    for i in range(parts):
        for copy in copies[i]:
            copy.wait()
        total = total + jnp.dot(columns_in[i], rows_in[i], preferred_element_type=f32)
    query[...] = total.astype(bf16)

    def tile_of(index, columns, count):
        here = pl.ds(pl.multiple_of(index * tile, tile), tile)
        q = query[here, columns]
        do = grad_out[here, columns]
        row = index * tile + lax.broadcasted_iota(jnp.int32, (tile, block), 0)
        column = lax.broadcasted_iota(jnp.int32, (tile, block), 1)
        scores = [
            lax.dot_general(q, keys[d][...], NT, preferred_element_type=f32) * scale
            for d in range(count)
        ]
        scores[0] = jnp.where(column <= row, scores[0], -1e30)
        highest = functools.reduce(
            jnp.maximum, [jnp.max(s, axis=1, keepdims=True) for s in scores]
        )
        weights = [jnp.exp(s - highest) for s in scores]
        inverse = 1.0 / functools.reduce(
            jnp.add, [jnp.sum(w, axis=1, keepdims=True) for w in weights]
        )
        probs = [w * inverse for w in weights]
        low = [p.astype(bf16) for p in probs]
        result = functools.reduce(
            jnp.add,
            [
                jnp.dot(low[d], values[d][...], preferred_element_type=f32)
                for d in range(count)
            ],
        ).astype(bf16)
        out[here, columns] = result
        correction = jnp.sum(do.astype(f32) * result.astype(f32), axis=1, keepdims=True)
        total = jnp.zeros((tile, size), f32)
        for d in range(count):
            grad_value[d] += lax.dot_general(low[d], do, TN, preferred_element_type=f32)
            grad_probs = lax.dot_general(do, values[d][...], NT, preferred_element_type=f32)
            grad_scores = (probs[d] * (grad_probs - correction)).astype(bf16)
            total = total + jnp.dot(grad_scores, keys[d][...], preferred_element_type=f32)
        grad_query[here, columns] = (total * scale).astype(bf16)

    for head in range(heads):
        columns = slice(head * size, (head + 1) * size)
        for count in range(1, blocks + 1):

            @pl.when(info[head] + 1 == count)
            def _(columns=columns, count=count):
                def step(index, carry):
                    tile_of(index, columns, count)
                    return carry

                lax.fori_loop(0, rows // tile, step, 0)


def attend(info, tokens, theirs, weight, start, grad_out, kv, tile=256, parts=8):
    rows, width = start.shape
    model = tokens.shape[1]
    size = kv.shape[-1]
    blocks, block = kv.shape[1:3]
    vmem = pl.BlockSpec(memory_space=pltpu.VMEM)
    return pl.pallas_call(
        functools.partial(attention_kernel, size ** (-0.5), tile),
        out_shape=(
            jax.ShapeDtypeStruct((rows, width), bf16),
            jax.ShapeDtypeStruct((rows, width), bf16),
            jax.ShapeDtypeStruct((blocks, block, size), f32),
        ),
        in_specs=[
            pl.BlockSpec(memory_space=pltpu.SMEM),
            pl.BlockSpec(memory_space=pl.ANY),
            pl.BlockSpec(memory_space=pl.ANY),
            pl.BlockSpec(memory_space=pl.ANY),
            vmem,
            vmem,
            vmem,
        ],
        out_specs=(vmem, vmem, vmem),
        scratch_shapes=[
            pltpu.VMEM((rows, width), bf16),
            pltpu.VMEM((parts, rows, model // parts), bf16),
            pltpu.VMEM((parts, model // parts, width), bf16),
            pltpu.SemaphoreType.DMA((3 * parts,)),
        ],
        compiler_params=pltpu.CompilerParams(vmem_limit_bytes=48 * 1024 * 1024),
        cost_estimate=pl.CostEstimate(
            flops=10 * rows * width * blocks * block + 2 * rows * width * model,
            bytes_accessed=16 * 1024 * 1024,
            transcendentals=rows * width // size * blocks * block,
        ),
        name="attention",
    )(info, tokens, theirs, weight, start, grad_out, kv)


def all_blocks_kernel(info, own, *refs):
    arrived, refs = refs[:-9], refs[-9:]
    up, low, rank_q, tokens, theirs, out, gradient, buffer, arrivals = refs
    core = info[0]
    size = gradient.shape[1]
    each = buffer.shape[-1] // size
    copies = []
    for block in range(out.shape[0]):
        part, lane = block // each, block % each * size
        columns = pl.ds(pl.multiple_of((2 * block + core) * size, size), size)
        target = buffer.at[part, :, pl.ds(lane, size)]
        copies.append(rows_of(tokens, theirs, columns, core, target, arrivals, 2 * block))
    for copy in sum(copies, []):
        copy.start()
    rows = gradient.shape[0]
    total = own[...]
    for other in arrived:
        total += other[...].astype(f32)
    total = total.astype(bf16)
    mine = total[:rows]
    gradient[...] = mine
    rank_v = lax.dot_general(up[...], mine, NT, preferred_element_type=f32).astype(bf16)
    ranks = jnp.concatenate([rank_q[...], rank_v], axis=0)
    up_part = lax.dot_general(low[...], mine, TN, preferred_element_type=f32).astype(bf16)
    bottom = ranks.shape[0]
    last = bottom + up_part.shape[0]
    for part in range(buffer.shape[0]):
        for copy in sum(copies[part * each : (part + 1) * each], []):
            copy.wait()
        product = jnp.dot(ranks, buffer[part], preferred_element_type=f32).astype(bf16)
        for j in range(each):
            block = part * each + j
            out[block, :bottom] = product[:, j * size : (j + 1) * size]
            out[block, bottom:last] = up_part
            out[block, last:] = total[rows:]


def all_blocks(info, own, arrived, up, low, rank_q, tokens, theirs, parts=4):
    rows, model = tokens.shape
    ranks, size = up.shape
    count = model // (2 * size)
    vmem = pl.BlockSpec(memory_space=pltpu.VMEM)
    anywhere = pl.BlockSpec(memory_space=pl.ANY)
    height = 3 * ranks + own.shape[0] - 2 * rows
    return pl.pallas_call(
        all_blocks_kernel,
        out_shape=(
            jax.ShapeDtypeStruct((count, height, size), bf16),
            jax.ShapeDtypeStruct((2 * rows, size), bf16),
        ),
        in_specs=[pl.BlockSpec(memory_space=pltpu.SMEM)]
        + [vmem] * (4 + len(arrived))
        + [anywhere, anywhere],
        out_specs=(vmem, vmem),
        scratch_shapes=[
            pltpu.VMEM((parts, 2 * rows, model // (2 * parts)), bf16),
            pltpu.SemaphoreType.DMA((2 * count,)),
        ],
        compiler_params=pltpu.CompilerParams(vmem_limit_bytes=56 * 1024 * 1024),
        cost_estimate=pl.CostEstimate(
            flops=4 * ranks * rows * model, bytes_accessed=3 * rows * model, transcendentals=0
        ),
        name="all_blocks",
    )(info, own, *arrived, up, low, rank_q, tokens, theirs)


def on_device(
    tokens,
    query_weight,
    key_weight,
    value_weight,
    adapter_down_weight,
    query_up_weight,
    value_up_weight,
    head_shifts,
    output_gradient,
):
    rows, model = tokens.shape
    heads = head_shifts.shape[0]
    width = query_weight.shape[1]
    size = width // heads
    half = width // 2
    depth = query_weight.shape[0]
    rank = adapter_down_weight.shape[1] // 2
    devices = lax.axis_size("ctx")
    chips = GROUP // (2 * rows)
    members = 2 * chips
    position = lax.axis_index("ctx")
    core = lax.rem(position, 2)
    chip = lax.rem(lax.div(position, 2), chips)
    plain = [[start + i for i in range(members)] for start in range(0, devices, members)]
    across = [[g[i] for g in plain] for i in range(members)]
    planes = devices // members

    def both(mine, theirs):
        return jnp.concatenate(
            [jnp.where(core == 0, mine, theirs), jnp.where(core == 0, theirs, mine)], axis=0
        )

    def half_of(array, which):
        return lax.dynamic_slice_in_dim(array, which * (array.shape[0] // 2), array.shape[0] // 2)

    theirs = to_chip(tokens, 0, True)
    grad_halves = output_gradient.reshape(rows, 2, half).transpose(1, 0, 2)
    grad_mine = lax.dynamic_index_in_dim(grad_halves, core, 0, keepdims=False)
    grad_away = lax.dynamic_index_in_dim(grad_halves, 1 - core, 0, keepdims=False)
    grad_out = both(grad_mine, to_chip(grad_away, 0, True))

    kv_rows = lax.all_to_all(
        payload(key_weight, value_weight, adapter_down_weight.T, members),
        "ctx", 0, 0, tiled=True, axis_index_groups=plain,
    )
    kv_rows = lax.all_gather(kv_rows, "ctx", axis=0, tiled=True, axis_index_groups=across)
    q_rows = jnp.stack([query_weight[:, :half], query_weight[:, half:]])
    q_rows = jnp.broadcast_to(q_rows[None], (chips, *q_rows.shape))
    q_rows = lax.all_to_all(
        q_rows.reshape(members, depth, half),
        "ctx", 0, 0, tiled=True, axis_index_groups=plain,
    )
    q_rows = lax.all_gather(
        q_rows.reshape(members * depth, half),
        "ctx", axis=0, tiled=True, axis_index_groups=across,
    )

    kv_weight = kv_rows.transpose(1, 0, 2).reshape(size + rank, model)
    mine = both(
        lax.dot_general(tokens, kv_weight, NT, preferred_element_type=f32),
        lax.dot_general(theirs, kv_weight, NT, preferred_element_type=f32),
    )
    low = mine[:, size:].astype(bf16)
    extra = jnp.dot(low, value_up_weight, preferred_element_type=f32)
    mine = (mine[:, :size] + jnp.where(core == 1, extra, 0.0)).astype(bf16)
    low_away = to_chip(low, 0, True)
    low_q = jnp.where(core == 0, low, low_away)
    low_v = jnp.where(core == 0, low_away, low)
    mine = jnp.stack([mine] + [to_chip(mine, d, False) for d in range(1, chips)])
    kv = jnp.stack([mine, to_chip(mine, 0, True)])

    up_mine = lax.dynamic_slice_in_dim(query_up_weight, core * half, half, axis=1)
    start = jnp.dot(low_q, up_mine, preferred_element_type=f32)
    shifts = lax.dynamic_slice_in_dim(head_shifts, core * (heads // 2), heads // 2)
    seen = jnp.where(shifts != 0, lax.rem(chip + chips // 2, chips), chip)
    info = jnp.concatenate([seen, core[None]]).astype(jnp.int32)
    output, grad_query, value_parts = attend(
        info, tokens, theirs, q_rows, start, grad_out, kv
    )

    attention_mine = half_of(output, core)
    attention_other = to_chip(half_of(output, 1 - core), 0, True)
    attention = jnp.concatenate(
        [
            jnp.where(core == 0, attention_mine, attention_other),
            jnp.where(core == 0, attention_other, attention_mine),
        ],
        axis=1,
    )

    count = value_parts.shape[0] * value_parts.shape[1]
    query_up_part = lax.dot_general(low_q, grad_query, TN, preferred_element_type=f32)
    rank_q = lax.dot_general(up_mine, grad_query, NT, preferred_element_type=f32)
    swapped = [value_parts, query_up_part, rank_q]
    swapped = jnp.concatenate([part.astype(bf16).reshape(-1, size) for part in swapped])
    swapped = [swapped, to_chip(swapped, 0, True)]
    value_parts = (swapped[0][:count].astype(f32) + swapped[1][:count].astype(f32)).reshape(
        value_parts.shape
    )
    last = count + rank * half // size
    rank_q = [part[last:].reshape(rank, -1).astype(f32) for part in swapped]
    rank_q = (rank_q[0] + rank_q[1]).astype(bf16)
    query_up_part = [part[count:last].reshape(rank, half) for part in swapped]
    query_up_part = jnp.concatenate(
        [jnp.where(core == 0, *query_up_part), jnp.where(core == 0, *query_up_part[::-1])], axis=1
    ).reshape(chips, -1, size)

    def with_share(d):
        share = lax.dynamic_index_in_dim(
            query_up_part, lax.rem(chip + chips - d, chips), 0, keepdims=False
        )
        return jnp.concatenate([value_parts[d].astype(bf16), share], axis=0)

    arrived = [to_chip(with_share(d), -d, False) for d in range(1, chips)]

    blocks, value_gradient = all_blocks(
        core[None].astype(jnp.int32),
        with_share(0).astype(f32),
        arrived,
        value_up_weight,
        low_v,
        rank_q,
        tokens,
        theirs,
    )
    same_core = [[i for i in range(devices) if i % 2 == c] for c in range(2)]
    blocks = lax.all_to_all(
        blocks, "ctx", 0, 0, tiled=True, axis_index_groups=same_core
    )
    copies, value_up_gradient, query_up = sum_blocks(
        blocks, rank, lax.axis_size("fsdp"), chips
    )
    copies = lax.all_to_all(copies, "fsdp", 0, 0, tiled=True)
    grad_down = jnp.sum(copies.astype(f32), axis=0)
    query_up_gradient = query_up.reshape(rank, width)
    return (
        attention,
        half_of(value_gradient, core),
        grad_down.T,
        query_up_gradient,
        value_up_gradient,
    )


def solution(mesh):
    in_specs = (
        P("ctx", None),
        P("ctx", "fsdp"),
        P("ctx", "fsdp"),
        P("ctx", "fsdp"),
        P("ctx", None),
        P(None, "fsdp"),
        P(None, "fsdp"),
        P("fsdp"),
        P("ctx", "fsdp"),
    )
    out_specs = (
        P("ctx", "fsdp"),
        P("ctx", "fsdp"),
        P("ctx", None),
        P(None, "fsdp"),
        P(None, "fsdp"),
    )
    return jax.shard_map(
        on_device, mesh=mesh, in_specs=in_specs, out_specs=out_specs, check_vma=False
    )
```

```python
import functools

import jax
import jax.numpy as jnp
from jax import lax
from jax.experimental import pallas as pl
from jax.experimental.pallas import tpu as pltpu
from jax.sharding import PartitionSpec as P

GROUP = 2048
bf16 = jnp.bfloat16
f32 = jnp.float32
NT = (((1,), (1,)), ((), ()))
TN = (((0,), (0,)), ((), ()))


def to_chip(value, chips, other_core):
    count = lax.axis_size("ctx")
    pairs = []
    for source in range(count):
        core = source % 2
        target = (source - core + 2 * chips) % count + (1 - core if other_core else core)
        pairs.append((source, target))
    return lax.ppermute(value, "ctx", pairs)


def payload_kernel(key_weight, value_weight, down, out):
    size, rank = key_weight.shape[1], down.shape[0] // 2
    adapters = down[...]
    for core, weight in enumerate((key_weight, value_weight)):
        turned = weight[...].astype(f32).T.astype(bf16)
        for member in range(core, out.shape[0], 2):
            out[member, :size] = turned
            out[member, size:] = adapters[core * rank : (core + 1) * rank]


def payload(key_weight, value_weight, down, members):
    depth, size = key_weight.shape
    vmem = pl.BlockSpec(memory_space=pltpu.VMEM)
    return pl.pallas_call(
        payload_kernel,
        out_shape=jax.ShapeDtypeStruct((members, size + down.shape[0] // 2, depth), bf16),
        in_specs=[vmem] * 3,
        out_specs=vmem,
        name="payload",
    )(key_weight, value_weight, down)


def rows_of(tokens, theirs, columns, core, target, arrivals, first):
    rows = tokens.shape[0]
    mine = target.at[pl.ds(pl.multiple_of(core * rows, rows), rows)]
    other = target.at[pl.ds(pl.multiple_of((1 - core) * rows, rows), rows)]
    return [
        pltpu.make_async_copy(tokens.at[:, columns], mine, arrivals.at[first]),
        pltpu.make_async_copy(theirs.at[:, columns], other, arrivals.at[first + 1]),
    ]


def attention_kernel(
    scale, tile, info, tokens, theirs, weight, start, grad_out, kv,
    out, grad_query, grad_value, query, columns_in, rows_in, arrivals,
):
    rows, size = query.shape[0], kv.shape[-1]
    heads = query.shape[1] // size
    blocks, block = kv.shape[1:3]
    keys = [kv.at[info[heads], d] for d in range(blocks)]
    values = [kv.at[1 - info[heads], d] for d in range(blocks)]
    parts, depth = rows_in.shape[:2]
    copies = []
    for i in range(parts):
        here = pl.ds(i * depth, depth)
        copies.append(
            rows_of(tokens, theirs, here, info[heads], columns_in.at[i], arrivals, 3 * i)
            + [pltpu.make_async_copy(weight.at[here], rows_in.at[i], arrivals.at[3 * i + 2])]
        )
    for copy in sum(copies, []):
        copy.start()
    grad_value[...] = jnp.zeros_like(grad_value)
    total = start[...]
    for i in range(parts):
        for copy in copies[i]:
            copy.wait()
        total = total + jnp.dot(columns_in[i], rows_in[i], preferred_element_type=f32)
    query[...] = total.astype(bf16)

    def tile_of(index, columns, count):
        here = pl.ds(pl.multiple_of(index * tile, tile), tile)
        q = query[here, columns]
        do = grad_out[here, columns]
        row = index * tile + lax.broadcasted_iota(jnp.int32, (tile, block), 0)
        column = lax.broadcasted_iota(jnp.int32, (tile, block), 1)
        scores = [
            lax.dot_general(q, keys[d][...], NT, preferred_element_type=f32) * scale
            for d in range(count)
        ]
        scores[0] = jnp.where(column <= row, scores[0], -1e30)
        highest = functools.reduce(
            jnp.maximum, [jnp.max(s, axis=1, keepdims=True) for s in scores]
        )
        weights = [jnp.exp(s - highest) for s in scores]
        inverse = 1.0 / functools.reduce(
            jnp.add, [jnp.sum(w, axis=1, keepdims=True) for w in weights]
        )
        probs = [w * inverse for w in weights]
        low = [p.astype(bf16) for p in probs]
        result = functools.reduce(
            jnp.add,
            [
                jnp.dot(low[d], values[d][...], preferred_element_type=f32)
                for d in range(count)
            ],
        ).astype(bf16)
        out[here, columns] = result
        correction = jnp.sum(do.astype(f32) * result.astype(f32), axis=1, keepdims=True)
        total = jnp.zeros((tile, size), f32)
        for d in range(count):
            grad_value[d] += lax.dot_general(low[d], do, TN, preferred_element_type=f32)
            grad_probs = lax.dot_general(do, values[d][...], NT, preferred_element_type=f32)
            grad_scores = (probs[d] * (grad_probs - correction)).astype(bf16)
            total = total + jnp.dot(grad_scores, keys[d][...], preferred_element_type=f32)
        grad_query[here, columns] = (total * scale).astype(bf16)

    for head in range(heads):
        columns = slice(head * size, (head + 1) * size)
        for count in range(1, blocks + 1):

            @pl.when(info[head] + 1 == count)
            def _(columns=columns, count=count):
                def step(index, carry):
                    tile_of(index, columns, count)
                    return carry

                lax.fori_loop(0, rows // tile, step, 0)


def attend(info, tokens, theirs, weight, start, grad_out, kv, tile=256, parts=8):
    rows, width = start.shape
    model = tokens.shape[1]
    size = kv.shape[-1]
    blocks, block = kv.shape[1:3]
    vmem = pl.BlockSpec(memory_space=pltpu.VMEM)
    return pl.pallas_call(
        functools.partial(attention_kernel, size ** (-0.5), tile),
        out_shape=(
            jax.ShapeDtypeStruct((rows, width), bf16),
            jax.ShapeDtypeStruct((rows, width), bf16),
            jax.ShapeDtypeStruct((blocks, block, size), f32),
        ),
        in_specs=[
            pl.BlockSpec(memory_space=pltpu.SMEM),
            pl.BlockSpec(memory_space=pl.ANY),
            pl.BlockSpec(memory_space=pl.ANY),
            pl.BlockSpec(memory_space=pl.ANY),
            vmem,
            vmem,
            vmem,
        ],
        out_specs=(vmem, vmem, vmem),
        scratch_shapes=[
            pltpu.VMEM((rows, width), bf16),
            pltpu.VMEM((parts, rows, model // parts), bf16),
            pltpu.VMEM((parts, model // parts, width), bf16),
            pltpu.SemaphoreType.DMA((3 * parts,)),
        ],
        compiler_params=pltpu.CompilerParams(vmem_limit_bytes=48 * 1024 * 1024),
        cost_estimate=pl.CostEstimate(
            flops=10 * rows * width * blocks * block + 2 * rows * width * model,
            bytes_accessed=16 * 1024 * 1024,
            transcendentals=rows * width // size * blocks * block,
        ),
        name="attention",
    )(info, tokens, theirs, weight, start, grad_out, kv)


def all_blocks_kernel(info, own, *refs):
    arrived, refs = refs[:-9], refs[-9:]
    up, low, rank_q, tokens, theirs, out, gradient, buffer, arrivals = refs
    core = info[0]
    size = gradient.shape[1]
    each = buffer.shape[-1] // size
    copies = []
    for block in range(out.shape[0]):
        part, lane = block // each, block % each * size
        columns = pl.ds(pl.multiple_of((2 * block + core) * size, size), size)
        target = buffer.at[part, :, pl.ds(lane, size)]
        copies.append(rows_of(tokens, theirs, columns, core, target, arrivals, 2 * block))
    for copy in sum(copies, []):
        copy.start()
    rows = gradient.shape[0]
    total = own[...]
    for other in arrived:
        total += other[...].astype(f32)
    total = total.astype(bf16)
    mine = total[:rows]
    gradient[...] = mine
    rank_v = lax.dot_general(up[...], mine, NT, preferred_element_type=f32).astype(bf16)
    ranks = jnp.concatenate([rank_q[...], rank_v], axis=0)
    up_part = lax.dot_general(low[...], mine, TN, preferred_element_type=f32).astype(bf16)
    bottom = ranks.shape[0]
    last = bottom + up_part.shape[0]
    for part in range(buffer.shape[0]):
        for copy in sum(copies[part * each : (part + 1) * each], []):
            copy.wait()
        product = jnp.dot(ranks, buffer[part], preferred_element_type=f32).astype(bf16)
        for j in range(each):
            block = part * each + j
            out[block, :bottom] = product[:, j * size : (j + 1) * size]
            out[block, bottom:last] = up_part
            out[block, last:] = total[rows:]


def all_blocks(info, own, arrived, up, low, rank_q, tokens, theirs, parts=4):
    rows, model = tokens.shape
    ranks, size = up.shape
    count = model // (2 * size)
    vmem = pl.BlockSpec(memory_space=pltpu.VMEM)
    anywhere = pl.BlockSpec(memory_space=pl.ANY)
    height = 3 * ranks + own.shape[0] - 2 * rows
    return pl.pallas_call(
        all_blocks_kernel,
        out_shape=(
            jax.ShapeDtypeStruct((count, height, size), bf16),
            jax.ShapeDtypeStruct((2 * rows, size), bf16),
        ),
        in_specs=[pl.BlockSpec(memory_space=pltpu.SMEM)]
        + [vmem] * (4 + len(arrived))
        + [anywhere, anywhere],
        out_specs=(vmem, vmem),
        scratch_shapes=[
            pltpu.VMEM((parts, 2 * rows, model // (2 * parts)), bf16),
            pltpu.SemaphoreType.DMA((2 * count,)),
        ],
        compiler_params=pltpu.CompilerParams(vmem_limit_bytes=56 * 1024 * 1024),
        cost_estimate=pl.CostEstimate(
            flops=4 * ranks * rows * model, bytes_accessed=3 * rows * model, transcendentals=0
        ),
        name="all_blocks",
    )(info, own, *arrived, up, low, rank_q, tokens, theirs)


def on_device(
    tokens,
    query_weight,
    key_weight,
    value_weight,
    adapter_down_weight,
    query_up_weight,
    value_up_weight,
    head_shifts,
    output_gradient,
):
    rows, model = tokens.shape
    heads = head_shifts.shape[0]
    width = query_weight.shape[1]
    size = width // heads
    half = width // 2
    depth = query_weight.shape[0]
    rank = adapter_down_weight.shape[1] // 2
    devices = lax.axis_size("ctx")
    chips = GROUP // (2 * rows)
    members = 2 * chips
    position = lax.axis_index("ctx")
    core = lax.rem(position, 2)
    chip = lax.rem(lax.div(position, 2), chips)
    plain = [[start + i for i in range(members)] for start in range(0, devices, members)]
    across = [[g[i] for g in plain] for i in range(members)]
    planes = devices // members

    def both(mine, theirs):
        return jnp.concatenate(
            [jnp.where(core == 0, mine, theirs), jnp.where(core == 0, theirs, mine)], axis=0
        )

    def half_of(array, which):
        return lax.dynamic_slice_in_dim(array, which * (array.shape[0] // 2), array.shape[0] // 2)

    theirs = to_chip(tokens, 0, True)
    grad_halves = output_gradient.reshape(rows, 2, half).transpose(1, 0, 2)
    grad_mine = lax.dynamic_index_in_dim(grad_halves, core, 0, keepdims=False)
    grad_away = lax.dynamic_index_in_dim(grad_halves, 1 - core, 0, keepdims=False)
    grad_out = both(grad_mine, to_chip(grad_away, 0, True))

    kv_rows = lax.all_to_all(
        payload(key_weight, value_weight, adapter_down_weight.T, members),
        "ctx", 0, 0, tiled=True, axis_index_groups=plain,
    )
    kv_rows = lax.all_gather(kv_rows, "ctx", axis=0, tiled=True, axis_index_groups=across)
    q_rows = jnp.stack([query_weight[:, :half], query_weight[:, half:]])
    q_rows = jnp.broadcast_to(q_rows[None], (chips, *q_rows.shape))
    q_rows = lax.all_to_all(
        q_rows.reshape(members, depth, half),
        "ctx", 0, 0, tiled=True, axis_index_groups=plain,
    )
    q_rows = lax.all_gather(
        q_rows.reshape(members * depth, half),
        "ctx", axis=0, tiled=True, axis_index_groups=across,
    )

    kv_weight = kv_rows.transpose(1, 0, 2).reshape(size + rank, model)
    mine = both(
        lax.dot_general(tokens, kv_weight, NT, preferred_element_type=f32),
        lax.dot_general(theirs, kv_weight, NT, preferred_element_type=f32),
    )
    low = mine[:, size:].astype(bf16)
    extra = jnp.dot(low, value_up_weight, preferred_element_type=f32)
    mine = (mine[:, :size] + jnp.where(core == 1, extra, 0.0)).astype(bf16)
    low_away = to_chip(low, 0, True)
    low_q = jnp.where(core == 0, low, low_away)
    low_v = jnp.where(core == 0, low_away, low)
    mine = jnp.stack([mine] + [to_chip(mine, d, False) for d in range(1, chips)])
    kv = jnp.stack([mine, to_chip(mine, 0, True)])

    up_mine = lax.dynamic_slice_in_dim(query_up_weight, core * half, half, axis=1)
    start = jnp.dot(low_q, up_mine, preferred_element_type=f32)
    shifts = lax.dynamic_slice_in_dim(head_shifts, core * (heads // 2), heads // 2)
    seen = jnp.where(shifts != 0, lax.rem(chip + chips // 2, chips), chip)
    info = jnp.concatenate([seen, core[None]]).astype(jnp.int32)
    output, grad_query, value_parts = attend(
        info, tokens, theirs, q_rows, start, grad_out, kv
    )

    attention_mine = half_of(output, core)
    attention_other = to_chip(half_of(output, 1 - core), 0, True)
    attention = jnp.concatenate(
        [
            jnp.where(core == 0, attention_mine, attention_other),
            jnp.where(core == 0, attention_other, attention_mine),
        ],
        axis=1,
    )

    count = value_parts.shape[0] * value_parts.shape[1]
    query_up_part = lax.dot_general(low_q, grad_query, TN, preferred_element_type=f32)
    rank_q = lax.dot_general(up_mine, grad_query, NT, preferred_element_type=f32)
    swapped = [value_parts, query_up_part, rank_q]
    swapped = jnp.concatenate([part.astype(bf16).reshape(-1, size) for part in swapped])
    swapped = [swapped, to_chip(swapped, 0, True)]
    value_parts = (swapped[0][:count].astype(f32) + swapped[1][:count].astype(f32)).reshape(
        value_parts.shape
    )
    last = count + rank * half // size
    rank_q = [part[last:].reshape(rank, -1).astype(f32) for part in swapped]
    rank_q = (rank_q[0] + rank_q[1]).astype(bf16)
    query_up_part = [part[count:last].reshape(rank, half) for part in swapped]
    query_up_part = jnp.concatenate(
        [jnp.where(core == 0, *query_up_part), jnp.where(core == 0, *query_up_part[::-1])], axis=1
    ).reshape(chips, -1, size)

    def with_share(d):
        share = lax.dynamic_index_in_dim(
            query_up_part, lax.rem(chip + chips - d, chips), 0, keepdims=False
        )
        return jnp.concatenate([value_parts[d].astype(bf16), share], axis=0)

    arrived = [to_chip(with_share(d), -d, False) for d in range(1, chips)]

    blocks, value_gradient = all_blocks(
        core[None].astype(jnp.int32),
        with_share(0).astype(f32),
        arrived,
        value_up_weight,
        low_v,
        rank_q,
        tokens,
        theirs,
    )
    same_core = [[i for i in range(devices) if i % 2 == c] for c in range(2)]
    blocks = lax.all_to_all(
        blocks, "ctx", 0, 0, tiled=True, axis_index_groups=same_core
    )
    summed = jnp.sum(blocks[:, : 3 * rank].astype(f32), axis=0)
    value_up_gradient = summed[2 * rank :]
    copies = jnp.broadcast_to(
        summed[None, : 2 * rank].astype(bf16), (lax.axis_size("fsdp"), 2 * rank, size)
    )
    copies = lax.all_to_all(copies, "fsdp", 0, 0, tiled=True)
    grad_down = jnp.sum(copies.astype(f32), axis=0)
    query_up = blocks[:, 3 * rank :].astype(f32)
    query_up = query_up.reshape(planes, chips, -1, size).sum(axis=0)
    query_up_gradient = query_up.reshape(rank, width)
    return (
        attention,
        half_of(value_gradient, core),
        grad_down.T,
        query_up_gradient,
        value_up_gradient,
    )


def solution(mesh):
    in_specs = (
        P("ctx", None),
        P("ctx", "fsdp"),
        P("ctx", "fsdp"),
        P("ctx", "fsdp"),
        P("ctx", None),
        P(None, "fsdp"),
        P(None, "fsdp"),
        P("fsdp"),
        P("ctx", "fsdp"),
    )
    out_specs = (
        P("ctx", "fsdp"),
        P("ctx", "fsdp"),
        P("ctx", None),
        P(None, "fsdp"),
        P(None, "fsdp"),
    )
    return jax.shard_map(
        on_device, mesh=mesh, in_specs=in_specs, out_specs=out_specs, check_vma=False
    )
```
